256 devices in a mesh: mesh: 32 (over x, z), harm: 8 (over y, core).
Axes of the slice: x: 4, y: 4, z: 8, core: 2. Of those that a mesh axis runs over, the one named last changes fastest.
Arguments:
- adjoint_rhs: float32 [16, 6, 2, 65536], P('harm', None, None, 'mesh'), may hold values from -20 to 20
- forward_field: float32 [16, 2, 65536], P('harm', None, 'mesh'), may hold values from -6 to 6
- stiffness: float32 [64, 64, 4096], P(None, None, 'mesh'), may hold values from -1 to 3, as said below
- mass_blocks: float32 [64, 64, 4096], P(None, None, 'mesh'), may hold values from -1 to 3, as said below
- frequency: float32 [16], P('harm'), may hold values from 0.25 to 4
- edge_mass: float32 [65536], P('mesh'), may hold values from 0.5 to 2
- connectivity: int32 [64, 4096], P(None, 'mesh'), may hold values from 0 to 3071, as said below
- send_list: int32 [32, 2, 512], P('mesh'), may hold values from -1 to 2047, as said below
- node_block: int32 [32768], P('mesh'), may hold values from 0 to 127
- node_shape: float32 [3, 64, 32768], P(None, None, 'mesh'), may hold values from -0.1875 to 0.1875
Outputs:
- adjoint: float32 [16, 6, 2, 65536], P('harm', None, None, 'mesh')
- shape_gradient: float32 [6, 3, 32768], P(None, None, ('mesh', 'harm'))
The draws below stay inside these ranges and needn't reach their ends.
Inputs may be any that keep to these rules, and one draw needn't show every extreme that they name: `stiffness`: each block is symmetric and its diagonal exceeds the sum of magnitudes of the other entries of its row. `mass_blocks`: each block is symmetric and its diagonal exceeds the sum of magnitudes of the other entries of its row. `send_list`: row 0 of a device lists owned edges shared with the device one lower along mesh, row 1 those shared with the device one higher; valid entries come first, then -1. A list holds at most 512 valid entries, and some device's row 0 and some device's row 1 hold exactly 512. The first device's row 0 and the last device's row 1 are empty. `connectivity`: an entry below 2048 is an edge the device owns; 2048 + k is entry k of the lower neighbour's row 1; 2560 + k is entry k of the upper neighbour's row 0. Only valid entries are named.
All inputs are finite; a program needn't handle non-finite values.
Results may differ from the reference program's by a relative error of at most 0.0003.
Values sent between devices are 32-bit elements; how exact they have to be, the bound alone decides.
No kernel may reach another device: no remote copies, remote signals or barrier semaphores. Data moves between devices by JAX's collectives and lax.ppermute only.
A program may use at most 128 MiB of HBM per device.

```python
import math
import jax
import jax.numpy as jnp
from jax import lax

EB = 64
HARMONICS = 16
FORCES = 6
ITERS = 3
BLK_DEV = 128
E_DEV = 2048
GMAX = 512
NODE_DEV = 1024
BLOCKS = 4096
EDGES = 65536
NODES = 32768
N_MESH = 32


def interface_plan(key):
    plan_key = jax.random.fold_in(key, 4411)
    count_key, rank_key, entry_key = jax.random.split(plan_key, 3)
    counts = jax.random.randint(count_key, (N_MESH, 2), GMAX // 4, GMAX + 1)
    device_rank = jnp.arange(N_MESH)
    chosen = jax.random.randint(rank_key, (2,), 0, N_MESH - 1)
    lower_counts = jnp.where(device_rank == chosen[1] + 1, GMAX, counts[:, 0])
    upper_counts = jnp.where(device_rank == chosen[0], GMAX, counts[:, 1])
    lower_counts = jnp.where(device_rank == 0, 0, lower_counts)
    upper_counts = jnp.where(device_rank == N_MESH - 1, 0, upper_counts)
    counts = jnp.stack([lower_counts, upper_counts], axis=1).astype(jnp.int32)
    entries = jax.random.randint(entry_key, (N_MESH, 2, GMAX), 0, E_DEV)
    is_valid = jnp.arange(GMAX)[None, None, :] < counts[:, :, None]
    lists = jnp.where(is_valid, entries, -1)
    return (counts, lists.astype(jnp.int32))


def draw_send_list(key, part):
    return interface_plan(key)[1]


def draw_connectivity(key, part):
    counts = interface_plan(key)[0]
    empty_count = jnp.zeros((1,), jnp.int32)
    from_lower = jnp.concatenate([empty_count, counts[:-1, 1]])
    from_upper = jnp.concatenate([counts[1:, 0], empty_count])
    conn_key = jax.random.fold_in(key, 5521)
    owned_key, raw_key, picker_key = jax.random.split(conn_key, 3)
    block_shape = (EB, N_MESH, BLK_DEV)
    owned = jax.random.randint(owned_key, block_shape, 0, E_DEV)
    raw_draw = jax.random.randint(raw_key, block_shape, 0, 1 << 20)
    picker = jax.random.randint(picker_key, block_shape, 0, 4)
    block_pos = jnp.arange(BLK_DEV)[None, None, :]
    slot_pos = jnp.arange(EB)[:, None, None]
    lower_in = from_lower[None, :, None]
    upper_in = from_upper[None, :, None]
    lower_zone = block_pos < BLK_DEV // 4
    upper_zone = block_pos >= BLK_DEV - BLK_DEV // 4
    lower_slot = E_DEV + raw_draw % jnp.maximum(lower_in, 1)
    upper_slot = E_DEV + GMAX + raw_draw % jnp.maximum(upper_in, 1)
    use_lower = lower_zone & (picker < 2) & (lower_in > 0)
    use_upper = upper_zone & (picker < 2) & (upper_in > 0)
    connect = jnp.where(use_lower, lower_slot, jnp.where(use_upper, upper_slot, owned))
    lower_top = (slot_pos == 0) & (block_pos == 0) & (lower_in > 0)
    upper_top = (slot_pos == 0) & (block_pos == BLK_DEV - 1) & (upper_in > 0)
    connect = jnp.where(lower_top, E_DEV + lower_in - 1, connect)
    connect = jnp.where(upper_top, E_DEV + GMAX + upper_in - 1, connect)
    return connect.reshape(EB, N_MESH * BLK_DEV).astype(jnp.int32)


def block_matrices(key, lowest, highest):
    off_key, diag_key = jax.random.split(key)
    raw_draw = jax.random.uniform(off_key, (EB, EB, BLOCKS), jnp.float32, -1.0, 1.0)
    symmetric = jnp.abs(raw_draw + jnp.transpose(raw_draw, (1, 0, 2))) * (0.5 / (EB - 1))
    diagonal = jax.random.uniform(diag_key, (EB, BLOCKS), jnp.float32, lowest, highest)
    is_diag = (jnp.arange(EB)[:, None] == jnp.arange(EB)[None, :])[:, :, None]
    return jnp.where(is_diag, diagonal[:, None, :], symmetric)


def draw_stiffness(key, part):
    return block_matrices(jax.random.fold_in(key, 6101), 1.05, 2.0)


def draw_mass_blocks(key, part):
    return block_matrices(jax.random.fold_in(key, 6203), 1.05, 3.0)


def draw_adjoint_rhs(key, part):
    full_shape = (HARMONICS, FORCES, 2, EDGES)
    second_key = jax.random.fold_in(jax.random.fold_in(key, 7307), 1)
    ramp = jnp.arange(EDGES, dtype=jnp.float32) / EDGES
    noise = jax.random.truncated_normal(second_key, -4.0, 4.0, full_shape, jnp.float32)
    return (noise + 1.0) * (0.3 * 10.0 ** ramp)


def touch_ends(values, own_key, low, largest):
    spot = [jax.random.randint(jax.random.fold_in(own_key, axis), (), 0, length) for axis, length in enumerate(values.shape)]
    main_axis = values.shape.index(max(values.shape))
    next_to = spot[:main_axis] + [(spot[main_axis] + 1) % values.shape[main_axis]] + spot[main_axis + 1:]
    return values.at[tuple(spot)].set(low).at[tuple(next_to)].set(largest)


def block_levels(own_key, dims, cuts, low, largest):
    factor_of, own = 1.0, jax.random.fold_in(own_key, 6)
    for axis_at, blocks in cuts:
        heights = jnp.exp(jax.random.uniform(jax.random.fold_in(own, axis_at), (blocks,), jnp.float32, low / len(cuts), largest / len(cuts)))
        factor_of = factor_of * jnp.repeat(heights, dims[axis_at] // blocks).reshape([-1 if axis == axis_at else 1 for axis in range(len(dims))])
    return factor_of


def scatter_about(key, extent, scale, limit, pieces=(), held_as=jnp.bfloat16):
    values = scale * jax.random.normal(key, extent, jnp.float32)
    if pieces:
        values = values * block_levels(key, extent, pieces, -0.22, 0.18)
    return jnp.clip(values, -limit, limit).astype(held_as)


def setup_inputs(seed: int = 0) -> dict:
    key_list = jax.random.split(jax.random.key(seed), 11)
    adjoint_rhs = draw_adjoint_rhs(jax.random.fold_in(key_list[10], 71), 0)
    forward_field = scatter_about(key_list[1], (HARMONICS, 2, EDGES), 1.0, 6.0, ((0, 8), (2, 32)), jnp.float32)
    stiffness = draw_stiffness(jax.random.fold_in(key_list[10], 71), 0)
    mass_blocks = draw_mass_blocks(jax.random.fold_in(key_list[10], 71), 0)
    frequency = jnp.clip(jnp.exp(math.log(4.0) - 2.7725887 * jax.random.uniform(key_list[4], (HARMONICS,), jnp.float32) ** block_levels(key_list[4], (HARMONICS,), ((0, 8),), -0.2, 0.2)), 0.25, 4.0)
    edge_mass = jnp.clip(jnp.exp(math.log(2.0) - 1.3862944 * jax.random.uniform(key_list[5], (EDGES,), jnp.float32) ** block_levels(key_list[5], (EDGES,), ((0, 32),), -0.2, 0.2)), 0.5, 2.0)
    connectivity = draw_connectivity(jax.random.fold_in(key_list[10], 71), 0)
    send_list = draw_send_list(jax.random.fold_in(key_list[10], 71), 0)
    node_block = touch_ends(jax.random.randint(key_list[8], (NODES,), 0, BLK_DEV), jax.random.fold_in(key_list[8], 1), 0, BLK_DEV - 1).astype(jnp.int32)
    node_shape = scatter_about(key_list[9], (3, EB, NODES), (EB * HARMONICS) ** -0.5, 0.1875, ((2, 32),), jnp.float32)
    return {"adjoint_rhs": adjoint_rhs, "forward_field": forward_field, "stiffness": stiffness, "mass_blocks": mass_blocks, "frequency": frequency, "edge_mass": edge_mass, "connectivity": connectivity, "send_list": send_list, "node_block": node_block, "node_shape": node_shape}


exact_mode = lax.Precision.HIGHEST


def global_edges(connectivity, send_list):
    device_rank = jnp.arange(N_MESH, dtype=jnp.int32)
    empty_list = jnp.full((1, GMAX), -1, jnp.int32)
    lower_lists = jnp.concatenate([empty_list, send_list[:-1, 1, :]], axis=0)
    upper_lists = jnp.concatenate([send_list[1:, 0, :], empty_list], axis=0)
    lower_global = jnp.where(lower_lists >= 0, (device_rank[:, None] - 1) * E_DEV + lower_lists, EDGES)
    upper_global = jnp.where(upper_lists >= 0, (device_rank[:, None] + 1) * E_DEV + upper_lists, EDGES)
    own_global = device_rank[:, None] * E_DEV + jnp.arange(E_DEV, dtype=jnp.int32)[None, :]
    extended = jnp.concatenate([own_global, lower_global, upper_global], axis=1).astype(jnp.int32)
    blocks_by_device = connectivity.reshape(EB, N_MESH, BLK_DEV).astype(jnp.int32)
    picked = extended[device_rank[None, :, None], blocks_by_device]
    return picked.reshape(EB, BLOCKS).astype(jnp.int32)


def block_apply(gathered, weight, stiffness, mass_blocks):
    first = jnp.einsum("ijb,...jb->...ib", stiffness, gathered, precision=exact_mode)
    second = jnp.einsum("ijb,...jb->...ib", mass_blocks, gathered, precision=exact_mode)
    return first + weight * second


def padded_gather(values, edge_ids):
    padded = jnp.concatenate([values, jnp.zeros(values.shape[:-1] + (1,), jnp.float32)], axis=-1)
    return padded[..., edge_ids]


def apply_operator(values, stiffness, mass_blocks, frequency, edge_mass, edge_ids):
    def one_harmonic(inputs):
        values_h, weight = inputs
        local_terms = block_apply(padded_gather(values_h, edge_ids), weight, stiffness, mass_blocks)
        totals = jnp.zeros(values_h.shape[:-1] + (EDGES + 1,), jnp.float32).at[..., edge_ids].add(local_terms)
        return totals[..., :EDGES] + weight * edge_mass * values_h

    return lax.map(one_harmonic, (values, frequency))


def reference(adjoint_rhs, forward_field, stiffness, mass_blocks, frequency, edge_mass, connectivity, send_list, node_block, node_shape):
    edge_ids = global_edges(connectivity, send_list)
    residual = adjoint_rhs
    direction = adjoint_rhs
    solution = jnp.zeros_like(adjoint_rhs)
    norm_now = jnp.sum(residual * residual)
    for iteration in range(ITERS):
        applied = apply_operator(direction, stiffness, mass_blocks, frequency, edge_mass, edge_ids)
        step_size = norm_now / jnp.sum(direction * applied)
        solution = solution + step_size * direction
        residual = residual - step_size * applied
        norm_next = jnp.sum(residual * residual)
        direction = residual + (norm_next / norm_now) * direction
        norm_now = norm_next

    def harmonic_term(carry, inputs):
        adjoint_h, field_h, weight = inputs
        field_terms = block_apply(padded_gather(field_h, edge_ids), weight, stiffness, mass_blocks)
        adjoint_blocks = padded_gather(adjoint_h, edge_ids)
        return carry + (adjoint_blocks[:, 0] * field_terms[0] - adjoint_blocks[:, 1] * field_terms[1]), None

    start_term = jnp.zeros((FORCES, EB, BLOCKS), jnp.float32)
    energy_term = lax.scan(harmonic_term, start_term, (solution, forward_field, frequency))[0]
    owner_rank = jnp.arange(NODES, dtype=jnp.int32) // NODE_DEV
    node_global = (owner_rank * BLK_DEV + node_block).astype(jnp.int32)
    at_nodes = energy_term[:, :, node_global]
    gradient = -jnp.einsum("kjn,ojn->okn", node_shape, at_nodes, precision=exact_mode)
    return solution, gradient
```

```python
import functools

import jax
import jax.numpy as jnp
from jax import lax
from jax.experimental import pallas as pl
from jax.experimental.pallas import tpu as pltpu
from jax.sharding import PartitionSpec as P

f32 = jnp.float32
bf16 = jnp.bfloat16
i32 = jnp.int32
LANES = 128
EDGES = 2048
SLOTS = 512
ROWS = 24
EB = 64
OWN_T, GHOST_T = EDGES // LANES, SLOTS // LANES
BOTH = ("mesh", "harm")

VMEM = pl.BlockSpec(memory_space=pltpu.VMEM)
SMEM = pl.BlockSpec(memory_space=pltpu.SMEM)


def kernel_call(body, name, out, specs, scratch=(), flops=0, nbytes=0):
    return pl.pallas_call(
        body,
        name=name,
        out_shape=out,
        in_specs=specs,
        out_specs=jax.tree.map(lambda _: VMEM, out),
        scratch_shapes=scratch,
        compiler_params=pltpu.CompilerParams(vmem_limit_bytes=48 * 2**20),
        cost_estimate=pl.CostEstimate(flops=flops, bytes_accessed=nbytes, transcendentals=0),
    )


def arr(*shape):
    return jax.ShapeDtypeStruct(shape, f32)


def lookup(tables, index):
    lane = jnp.broadcast_to(index & (LANES - 1), (8, LANES))
    high = jnp.broadcast_to(index >> 7, (8, LANES))
    found = [jnp.take_along_axis(t, lane, axis=1, mode="promise_in_bounds") for t in tables]
    bit = 1
    while len(found) > 1:
        odd = (high & bit) != 0
        found = [
            jnp.where(odd, found[a + 1], found[a]) if a + 1 < len(found) else found[a]
            for a in range(0, len(found), 2)
        ]
        bit *= 2
    return found[0]


def tiles(ref, row, count):
    return [ref[row : row + 8, t * LANES : (t + 1) * LANES] for t in range(count)]


def gather_blocks(own, low, up, conn, out, groups):
    def body(j, carry):
        index = conn[pl.ds(j, 1), :]
        for q, g in enumerate(groups):
            tables = tiles(own, g * 8, OWN_T) + tiles(low, g * 8, GHOST_T) + tiles(up, g * 8, GHOST_T)
            out[j, q * 8 : q * 8 + 8, :] = lookup(tables, index)
        return carry

    lax.fori_loop(0, EB, body, 0, unroll=4)


def product(freq, got, stiff, mass, out, per_harm, wide):
    for h in range(2):
        weight = freq[h]

        def outer(jt, carry):
            def inner(i, sums):
                ks = []
                for q in range(wide):
                    rows = pl.ds(pl.multiple_of((jt * wide + q) * 8, 8), 8)
                    ks.append(stiff[i, rows, :] + weight * mass[i, rows, :])
                new = []
                for r in range(per_harm):
                    x = jnp.broadcast_to(got[i, pl.ds(h * per_harm + r, 1), :], (8, LANES))
                    for q in range(wide):
                        new.append(sums[r * wide + q] + ks[q] * x)
                return tuple(new)

            zero = jnp.zeros((8, LANES), f32)
            sums = lax.fori_loop(0, EB, inner, (zero,) * (per_harm * wide), unroll=4)
            for r in range(per_harm):
                for q in range(wide):
                    rows = pl.ds(pl.multiple_of((jt * wide + q) * 8, 8), 8)
                    out[h * per_harm + r, rows, :] = sums[r * wide + q]
            return carry

        lax.fori_loop(0, EB // (8 * wide), outer, 0)


def pieces(x):
    high = x.astype(bf16).astype(f32)
    return jnp.concatenate([high, x - high], axis=0).astype(bf16)


def one_hot_low(index):
    low = jnp.broadcast_to(index & 255, (256, LANES))
    return jnp.where(low == lax.broadcasted_iota(i32, (256, LANES), 0), 1.0, 0.0).astype(bf16)


def masked_stack(parts, index, count):
    high = index >> 8
    stack = []
    for t in range(count):
        mask = jnp.broadcast_to(jnp.where(high == t, 1.0, 0.0), parts.shape).astype(bf16)
        stack.append(parts * mask)
    return stack


def add_up(stack, hot):
    return lax.dot_general(stack, hot, (((1,), (1,)), ((), ())), preferred_element_type=f32)


def scatter_blocks(terms, conn, stack, hot, total):
    chunk = 16
    total[...] = jnp.zeros_like(total)

    def outer(c, carry):
        def body(jj, inner):
            j = c * chunk + jj
            index = conn[pl.ds(j, 1), :]
            cols = pl.ds(pl.multiple_of(jj * LANES, LANES), LANES)
            hot[:, cols] = one_hot_low(index)
            x = terms[:, pl.ds(j, 1), :].reshape(ROWS, LANES)
            for t, part in enumerate(masked_stack(pieces(x), index, 12)):
                stack[t * 48 : t * 48 + 48, cols] = part
            return inner

        lax.fori_loop(0, chunk, body, 0, unroll=2)
        total[...] += add_up(stack[...], hot[...])
        return carry

    lax.fori_loop(0, EB // chunk, outer, 0)


def total_tile(total, t):
    return total[t * 48 : t * 48 + 24, :] + total[t * 48 + 24 : t * 48 + 48, :]


def transposed_lists(rim):
    columns = jnp.transpose(rim[24:32, :])
    return columns[:, 4:5], columns[:, 5:6]


def finish(p, lists, rim_low, rim_up, my_low, my_up, from_low, from_up, far_low, far_up, own, low, up):
    arrived = jnp.concatenate([from_low[24:48, :], from_up[24:48, :]], axis=1)
    hots, stacks = [], []
    for c in range(2 * GHOST_T):
        index = lists[c // GHOST_T : c // GHOST_T + 1, (c % GHOST_T) * LANES : (c % GHOST_T + 1) * LANES]
        hots.append(one_hot_low(index))
        parts = pieces(arrived[:, c * LANES : (c + 1) * LANES])
        stacks.append(jnp.concatenate(masked_stack(parts, index, 8), axis=0))
    sums = add_up(jnp.concatenate(stacks, axis=1), jnp.concatenate(hots, axis=1))
    for t in range(8):
        own[0:24, t * 256 : (t + 1) * 256] = p[:, t * 256 : (t + 1) * 256] + total_tile(sums, t)

    for rim, row, first, second, sent, out in (
        (rim_low, 29, far_low[...], my_low[...], from_low, low),
        (rim_up, 28, my_up[...], far_up[...], from_up, up),
    ):
        listed = rim[row : row + 1, :]
        ghosts = sent[0:24, :]
        for column, values in zip(transposed_lists(rim), (first, second)):
            match = jnp.where(column == listed, 1.0, 0.0).astype(bf16)
            both = jnp.dot(pieces(values), match, preferred_element_type=f32)
            ghosts = ghosts + both[0:24] + both[24:48]
        out[0:24, :] = ghosts


def edge_weights(freq, rows, width):
    upper = lax.broadcasted_iota(i32, (rows, width), 0) < rows // 2
    return jnp.where(upper, freq[0], freq[1])


def partial_outputs(freq, own, mass_row, lists, total, p, to_low, to_up, far_to_low, far_to_up):
    weights = edge_weights(freq, ROWS, 256)
    for t in range(8):
        cols = slice(t * 256, (t + 1) * 256)
        p[:, cols] = total_tile(total, t) + weights * mass_row[0:1, cols] * own[0:24, cols]
    for t in range(2):
        cols = slice(t * 256, (t + 1) * 256)
        low, up = total_tile(total, 8 + t), total_tile(total, 10 + t)
        to_low[24:48, cols] = low
        far_to_low[:, cols] = low
        to_up[24:48, cols] = up
        far_to_up[:, cols] = up
    pick_listed(p, lists, (to_low, to_up), 3)


def pick_listed(source, lists, outs, groups):
    for side in range(2):
        for c in range(GHOST_T):
            cols = slice(c * LANES, (c + 1) * LANES)
            index = lists[side : side + 1, cols]
            for g in range(groups):
                value = lookup(tiles(source, g * 8, OWN_T), index)
                outs[side][g * 8 : g * 8 + 8, cols] = jnp.where(index >= 0, value, 0.0)


def fold(x):
    rows, cols = x.shape
    total = jnp.zeros((8, LANES), f32)
    for r in range(rows // 8):
        for c in range(cols // LANES):
            total = total + x[r * 8 : r * 8 + 8, c * LANES : (c + 1) * LANES]
    return total


def prep_kernel(rhs, field, lists, rows, to_low, to_up):
    for h in range(2):
        for o in range(6):
            at = h * 12 + o * 2
            rows[at : at + 2, :] = rhs[h, o]
        rows[24 + 2 * h : 26 + 2 * h, :] = field[h]
    rows[28:32, :] = jnp.zeros((4, EDGES), f32)
    pick_listed(rows, lists, (to_low, to_up), 4)
    for out in (to_low, to_up):
        out[28:30, :] = lists[...].astype(f32)


def first_kernel(
    freq, rows, low, up, conn, lists, stiff, mass, mass_row,
    p, to_low, to_up, far_to_low, far_to_up, got, terms, stack, hot, total,
):
    gather_blocks(rows, low, up, conn, got, (0, 1, 2))
    product(freq, got, stiff, mass, terms, 12, 2)
    scatter_blocks(terms, conn, stack, hot, total)
    partial_outputs(freq, rows, mass_row, lists, total, p, to_low, to_up, far_to_low, far_to_up)


def second_kernel(
    freq, rows, rim_low, rim_up, conn, lists, stiff, mass, mass_row,
    p, my_low, my_up, from_low, from_up, far_low, far_up,
    p2, to_low, to_up, far_to_low, far_to_up, got, own, moments, low, up, terms, stack, hot, total,
):
    finish(p, lists, rim_low, rim_up, my_low, my_up, from_low, from_up, far_low, far_up, own, low, up)
    b, w = rows[0:24, :], own[...]
    moments[0:8, :] = fold(b * b)
    moments[8:16, :] = fold(b * w)
    moments[16:24, :] = fold(w * w)
    gather_blocks(own, low, up, conn, got, (0, 1, 2))
    product(freq, got, stiff, mass, terms, 12, 2)
    scatter_blocks(terms, conn, stack, hot, total)
    partial_outputs(freq, own, mass_row, lists, total, p2, to_low, to_up, far_to_low, far_to_up)


def quadratic(freq, got, got_rows, stiff, mass):
    result = jnp.zeros((8, LANES), f32)
    for h in range(2):
        weight = freq[h]
        for jt in range(8):

            def inner(i, sums, scale=1.0):
                k = stiff[i, jt * 8 : jt * 8 + 8, :] + weight * mass[i, jt * 8 : jt * 8 + 8, :]
                return tuple(
                    s + k * jnp.broadcast_to(got[i, h * 12 + r : h * 12 + r + 1, :], (8, LANES))
                    for r, s in enumerate(sums)
                )

            zero = jnp.zeros((8, LANES), f32)
            sums = (zero,) * 12
            if jt < 7:
                sums = lax.fori_loop(jt * 8 + 8, EB, inner, sums, unroll=4)
                sums = tuple(s + s for s in sums)
            sums = lax.fori_loop(jt * 8, jt * 8 + 8, inner, sums, unroll=4)
            for r in range(12):
                mine = got_rows[pl.ds(jt * 8 * ROWS + h * 12 + r, 8, stride=ROWS), :]
                result = result + sums[r] * mine
    return result


def third_kernel(
    count, freq, rim_low, rim_up, conn, lists, stiff, mass, mass_row,
    p, my_low, my_up, from_low, from_up, far_low, far_up, w_ref, early,
    got_out, own, message, low, up, got,
):
    finish(p, lists, rim_low, rim_up, my_low, my_up, from_low, from_up, far_low, far_up, own, low, up)
    gather_blocks(own, low, up, conn, got, (0, 1, 2))
    got_rows = got_out
    for j in range(EB):
        got_rows[j * ROWS : (j + 1) * ROWS, :] = got[j]
    w, v = w_ref[...], own[...]
    last = quadratic(freq, got, got_rows, stiff, mass)
    weights = edge_weights(freq, ROWS, 256)
    for t in range(8):
        cols = slice(t * 256, (t + 1) * 256)
        last = last + fold(weights * mass_row[0:1, cols] * v[:, cols] * v[:, cols])
    tiles_of = [early[0:8, :], early[8:16, :], early[16:24, :], fold(w * v), fold(v * v), last]
    lane = lax.broadcasted_iota(i32, (1, LANES), 1)
    line = jnp.zeros((1, LANES), f32)
    for k, tile in enumerate(tiles_of):
        line = line + jnp.where(lane == k, jnp.sum(tile), 0.0)
    message[...] = jnp.broadcast_to(line, (count, LANES))


def field_kernel(freq, rows, low, up, conn, stiff, mass, y, got):
    gather_blocks(rows, low, up, conn, got, (3,))
    product(freq, got, stiff, mass, y, 2, 4)


def gradients(got_rows, y, node_block, node_shape, energy, out, base):
    for jt in range(8):
        ys = [y[r, jt * 8 : jt * 8 + 8, :] for r in range(4)]
        for o in range(6):
            term = jnp.zeros((8, LANES), f32)
            for h in range(2):
                for c in range(2):
                    x = got_rows[pl.ds(jt * 8 * ROWS + h * 12 + o * 2 + c, 8, stride=ROWS), :]
                    term = term - x * ys[h * 2 + c] if c else term + x * ys[h * 2 + c]
            energy[o, jt * 8 : jt * 8 + 8, :] = term

    def body(c, carry):
        index = jnp.broadcast_to(node_block[pl.ds(c, 1), :], (8, LANES))
        cols = pl.ds(pl.multiple_of(c * LANES, LANES), LANES)
        sums = [jnp.zeros((8, LANES), f32) for _ in range(18)]
        for jt in range(8):
            shape = [node_shape[k, jt * 8 : jt * 8 + 8, cols] for k in range(3)]
            for o in range(6):
                x = jnp.take_along_axis(energy[o, jt * 8 : jt * 8 + 8, :], index, axis=1, mode="promise_in_bounds")
                for k in range(3):
                    sums[o * 3 + k] = sums[o * 3 + k] - shape[k] * x
        for q in range(18):
            out[c, base + q : base + q + 1, :] = jnp.sum(sums[q], axis=0, keepdims=True)
        return carry

    lax.fori_loop(0, 8, body, 0)


def early_gradient_kernel(got0, got1, y, node_block, node_shape, out, energy):
    gradients(got0, y, node_block, node_shape, energy, out, 0)
    gradients(got1, y, node_block, node_shape, energy, out, 18)
    out[:, 36:40, :] = jnp.zeros((8, 4, LANES), f32)


def late_gradient_kernel(early, got2, y, node_block, node_shape, out, energy):
    out[:, 0:40, :] = early[...]
    gradients(got2, y, node_block, node_shape, energy, out, 40)
    out[:, 58:64, :] = jnp.zeros((8, 6, LANES), f32)


def last_kernel(messages, rows, w, v, shares, adjoint, gradient):
    line = jnp.sum(messages[...], axis=0, keepdims=True)
    lane = lax.broadcasted_iota(i32, (1, LANES), 1)

    def moment(k):
        return jnp.sum(jnp.where(lane == k, line, 0.0), axis=1, keepdims=True)

    m = [moment(k) for k in range(6)]
    a0 = m[0] / m[1]
    r1 = (None, -a0)
    rr1 = m[0] - 2.0 * a0 * m[1] + a0 * a0 * m[2]
    b0 = rr1 / m[0]
    d1 = (1.0 + b0, -a0)
    dad1 = d1[0] * d1[0] * m[1] + 2.0 * d1[0] * d1[1] * m[2] + d1[1] * d1[1] * m[3]
    a1 = rr1 / dad1
    r2 = (None, r1[1] - a1 * d1[0], -a1 * d1[1])
    rr2 = (
        m[0] + 2.0 * r2[1] * m[1] + (2.0 * r2[2] + r2[1] * r2[1]) * m[2]
        + 2.0 * r2[1] * r2[2] * m[3] + r2[2] * r2[2] * m[4]
    )
    b1 = rr2 / rr1
    d2 = (1.0 + b1 * d1[0], r2[1] + b1 * d1[1], r2[2])
    dad2 = (
        d2[0] * d2[0] * m[1] + 2.0 * d2[0] * d2[1] * m[2] + (2.0 * d2[0] * d2[2] + d2[1] * d2[1]) * m[3]
        + 2.0 * d2[1] * d2[2] * m[4] + d2[2] * d2[2] * m[5]
    )
    a2 = rr2 / dad2
    c0 = a0 + a1 * d1[0] + a2 * d2[0]
    c1 = a1 * d1[1] + a2 * d2[1]
    c2 = a2 * d2[2]
    for h in range(2):
        for o in range(6):
            at = slice(h * 12 + o * 2, h * 12 + o * 2 + 2)
            adjoint[h, o] = c0 * rows[at, :] + c1 * w[at, :] + c2 * v[at, :]
    share = shares[0]
    for d in range(1, 8):
        share = share + shares[d]
    for o in range(6):
        gradient[o] = (
            c0 * share[o * 3 : o * 3 + 3] + c1 * share[18 + o * 3 : 21 + o * 3] + c2 * share[40 + o * 3 : 43 + o * 3]
        )


def shifted(x, by):
    count = lax.axis_size("mesh")
    return lax.ppermute(x, "mesh", [(i, i + by) for i in range(count) if 0 <= i + by < count])


def per_device(
    adjoint_rhs, forward_field, stiffness, mass_blocks, frequency, edge_mass, connectivity, send_list, node_block, node_shape
):
    lists = send_list[0]
    mass_row = edge_mass.reshape(1, EDGES)
    nodes = node_block.reshape(8, LANES)
    count = lax.axis_size("mesh") * lax.axis_size("harm")
    block_scratch = [
        pltpu.VMEM((ROWS, EB, LANES), f32),
        pltpu.VMEM((12 * 48, 16 * LANES), bf16),
        pltpu.VMEM((256, 16 * LANES), bf16),
        pltpu.VMEM((12 * 48, 256), f32),
    ]
    ghost = pltpu.VMEM((ROWS, SLOTS), f32)

    rows, to_low, to_up = kernel_call(
        prep_kernel, "prep", (arr(32, EDGES), arr(32, SLOTS), arr(32, SLOTS)), [VMEM] * 3, flops=10**6, nbytes=10**6
    )(adjoint_rhs, forward_field, lists)
    rim_low, rim_up = shifted(to_up, 1), shifted(to_low, -1)

    sums = (arr(ROWS, EDGES), arr(48, SLOTS), arr(48, SLOTS), arr(ROWS, SLOTS), arr(ROWS, SLOTS))
    p, to_low, to_up, far_to_low, far_to_up, got0 = kernel_call(
        first_kernel, "first", sums + (arr(EB, ROWS, LANES),), [SMEM] + [VMEM] * 8, block_scratch,
        flops=10**8, nbytes=10**7,
    )(frequency, rows, rim_low, rim_up, connectivity, lists, stiffness, mass_blocks, mass_row)

    def exchange():
        return (
            far_to_low, far_to_up, shifted(to_up, 1), shifted(to_low, -1), shifted(far_to_up, 2), shifted(far_to_low, -2)
        )

    arrived = exchange()
    (y,) = kernel_call(
        field_kernel, "field", (arr(4, EB, LANES),), [SMEM] + [VMEM] * 6, [pltpu.VMEM((EB, 8, LANES), f32)],
        flops=10**8, nbytes=10**7,
    )(frequency, rows, rim_low, rim_up, connectivity, stiffness, mass_blocks)

    p, to_low, to_up, far_to_low, far_to_up, got1, w, early = kernel_call(
        second_kernel, "second", sums + (arr(EB, ROWS, LANES), arr(ROWS, EDGES), arr(24, LANES)),
        [SMEM] + [VMEM] * 15, [ghost, ghost] + block_scratch, flops=10**8, nbytes=10**7,
    )(
        frequency, rows, rim_low, rim_up, connectivity, lists, stiffness, mass_blocks, mass_row, p, *arrived
    )

    arrived = exchange()
    flat = lambda x: x.reshape(EB * ROWS, LANES)
    (grads,) = kernel_call(
        early_gradient_kernel, "early_gradient", (arr(8, 40, LANES),), [VMEM] * 5, [pltpu.VMEM((6, EB, LANES), f32)],
        flops=10**8, nbytes=10**7,
    )(flat(got0), flat(got1), y, nodes, node_shape)

    got2, v, message = kernel_call(
        functools.partial(third_kernel, count), "third", (arr(EB * ROWS, LANES), arr(ROWS, EDGES), arr(count, LANES)),
        [SMEM] + [VMEM] * 16, [ghost, ghost, pltpu.VMEM((EB, ROWS, LANES), f32)], flops=10**8, nbytes=10**7,
    )(
        frequency, rim_low, rim_up, connectivity, lists, stiffness, mass_blocks, mass_row, p, *arrived, w, early
    )
    messages = lax.all_to_all(message, BOTH, 0, 0, tiled=True)
    (grads,) = kernel_call(
        late_gradient_kernel, "late_gradient", (arr(8, 64, LANES),), [VMEM] * 5, [pltpu.VMEM((6, EB, LANES), f32)],
        flops=10**8, nbytes=10**7,
    )(grads, got2, y, nodes, node_shape)
    shares = lax.all_to_all(grads, "harm", 0, 0, tiled=True)
    adjoint, gradient = kernel_call(
        last_kernel, "last", (arr(*adjoint_rhs.shape), arr(6, 3, LANES)), [VMEM] * 5, flops=10**6, nbytes=10**6
    )(messages, rows, w, v, shares)
    return adjoint, gradient


def solution(mesh):
    return jax.shard_map(
        per_device,
        mesh=mesh,
        in_specs=(
            P("harm", None, None, "mesh"),
            P("harm", None, "mesh"),
            P(None, None, "mesh"),
            P(None, None, "mesh"),
            P("harm"),
            P("mesh"),
            P(None, "mesh"),
            P("mesh", None, None),
            P("mesh"),
            P(None, None, "mesh"),
        ),
        out_specs=(P("harm", None, None, "mesh"), P(None, None, ("mesh", "harm"))),
        check_vma=False,
    )
```

```python
import functools

import jax
import jax.numpy as jnp
from jax import lax
from jax.experimental import pallas as pl
from jax.experimental.pallas import tpu as pltpu
from jax.sharding import PartitionSpec as P

f32 = jnp.float32
bf16 = jnp.bfloat16
i32 = jnp.int32
LANES = 128
EDGES = 2048
SLOTS = 512
ROWS = 24
EB = 64
OWN_T, GHOST_T = EDGES // LANES, SLOTS // LANES
BOTH = ("mesh", "harm")

VMEM = pl.BlockSpec(memory_space=pltpu.VMEM)
SMEM = pl.BlockSpec(memory_space=pltpu.SMEM)


def kernel_call(body, name, out, specs, scratch=(), flops=0, nbytes=0):
    return pl.pallas_call(
        body,
        name=name,
        out_shape=out,
        in_specs=specs,
        out_specs=jax.tree.map(lambda _: VMEM, out),
        scratch_shapes=scratch,
        compiler_params=pltpu.CompilerParams(vmem_limit_bytes=20 * 2**20),
        cost_estimate=pl.CostEstimate(flops=flops, bytes_accessed=nbytes, transcendentals=0),
    )


def arr(*shape):
    return jax.ShapeDtypeStruct(shape, f32)


def lookup(tables, index):
    lane = jnp.broadcast_to(index & (LANES - 1), (8, LANES))
    high = jnp.broadcast_to(index >> 7, (8, LANES))
    found = [jnp.take_along_axis(t, lane, axis=1, mode="promise_in_bounds") for t in tables]
    bit = 1
    while len(found) > 1:
        odd = (high & bit) != 0
        found = [
            jnp.where(odd, found[a + 1], found[a]) if a + 1 < len(found) else found[a]
            for a in range(0, len(found), 2)
        ]
        bit *= 2
    return found[0]


def tiles(ref, row, count):
    return [ref[row : row + 8, t * LANES : (t + 1) * LANES] for t in range(count)]


def gather_own(own, conn, out, groups):
    def body(j, carry):
        index = conn[pl.ds(j, 1), :]
        for q, g in enumerate(groups):
            out[j, q * 8 : q * 8 + 8, :] = lookup(tiles(own, g * 8, OWN_T), index)
        return carry

    lax.fori_loop(0, EB, body, 0, unroll=4)


def gather_ghosts(got_own, low, up, conn, out, groups):
    def body(j, carry):
        index = conn[pl.ds(j, 1), :]
        ghost = jnp.broadcast_to(index >= EDGES, (8, LANES))
        for q, g in enumerate(groups):
            value = lookup(tiles(low, g * 8, GHOST_T) + tiles(up, g * 8, GHOST_T), index)
            out[j, q * 8 : q * 8 + 8, :] = jnp.where(ghost, value, got_own[j, q * 8 : q * 8 + 8, :])
        return carry

    lax.fori_loop(0, EB, body, 0, unroll=4)


def product(freq, got, stiff, mass, out, per_harm, wide):
    for h in range(2):
        weight = freq[h]

        def outer(jt, carry):
            def inner(i, sums):
                ks = []
                for q in range(wide):
                    rows = pl.ds(pl.multiple_of((jt * wide + q) * 8, 8), 8)
                    ks.append(stiff[i, rows, :] + weight * mass[i, rows, :])
                new = []
                for r in range(per_harm):
                    x = jnp.broadcast_to(got[i, pl.ds(h * per_harm + r, 1), :], (8, LANES))
                    for q in range(wide):
                        new.append(sums[r * wide + q] + ks[q] * x)
                return tuple(new)

            zero = jnp.zeros((8, LANES), f32)
            sums = lax.fori_loop(0, EB, inner, (zero,) * (per_harm * wide), unroll=4)
            for r in range(per_harm):
                for q in range(wide):
                    rows = pl.ds(pl.multiple_of((jt * wide + q) * 8, 8), 8)
                    out[h * per_harm + r, rows, :] = sums[r * wide + q]
            return carry

        lax.fori_loop(0, EB // (8 * wide), outer, 0)


def pieces(x):
    high = x.astype(bf16).astype(f32)
    return jnp.concatenate([high, x - high], axis=0).astype(bf16)


def one_hot_low(index):
    low = jnp.broadcast_to(index & 255, (256, LANES))
    return jnp.where(low == lax.broadcasted_iota(i32, (256, LANES), 0), 1.0, 0.0).astype(bf16)


def masked_stack(parts, index, first, last):
    high = index >> 8
    stack = []
    for t in range(first, last):
        mask = jnp.broadcast_to(jnp.where(high == t, 1.0, 0.0), parts.shape).astype(bf16)
        stack.append(parts * mask)
    return stack


def add_up(stack, hot):
    return lax.dot_general(stack, hot, (((1,), (1,)), ((), ())), preferred_element_type=f32)


CHUNK = 16


def scatter_blocks(terms, conn, hot, stack, total, first, last):
    total[...] = jnp.zeros_like(total)

    def outer(c, carry):
        def body(jj, inner):
            j = c * CHUNK + jj
            index = conn[pl.ds(j, 1), :]
            cols = pl.ds(pl.multiple_of(jj * LANES, LANES), LANES)
            x = terms[:, pl.ds(j, 1), :].reshape(ROWS, LANES)
            for t, part in enumerate(masked_stack(pieces(x), index, first, last)):
                stack[t * 48 : t * 48 + 48, cols] = part
            return inner

        lax.fori_loop(0, CHUNK, body, 0, unroll=2)
        wide = CHUNK * LANES
        total[...] += add_up(stack[...], hot[:, pl.ds(pl.multiple_of(c * wide, wide), wide)])
        return carry

    lax.fori_loop(0, EB // CHUNK, outer, 0)


def total_tile(total, t):
    return total[t * 48 : t * 48 + 24, :] + total[t * 48 + 24 : t * 48 + 48, :]


def edge_weights(freq, rows, width):
    upper = lax.broadcasted_iota(i32, (rows, width), 0) < rows // 2
    return jnp.where(upper, freq[0], freq[1])


def pick_listed(source, lists, outs, groups):
    for side in range(2):
        for c in range(GHOST_T):
            cols = slice(c * LANES, (c + 1) * LANES)
            index = lists[side : side + 1, cols]
            for g in range(groups):
                value = lookup(tiles(source, g * 8, OWN_T), index)
                outs[side][g * 8 : g * 8 + 8, cols] = jnp.where(index >= 0, value, 0.0)


def fold(x):
    rows, cols = x.shape
    total = jnp.zeros((8, LANES), f32)
    for r in range(rows // 8):
        for c in range(cols // LANES):
            total = total + x[r * 8 : r * 8 + 8, c * LANES : (c + 1) * LANES]
    return total


def prep_kernel(rhs, field, lists, rows, to_low, to_up):
    for h in range(2):
        for o in range(6):
            at = h * 12 + o * 2
            rows[at : at + 2, :] = rhs[h, o]
        rows[24 + 2 * h : 26 + 2 * h, :] = field[h]
    rows[28:32, :] = jnp.zeros((4, EDGES), f32)
    pick_listed(rows, lists, (to_low, to_up), 4)


def hot_kernel(conn, hot):
    def body(j, carry):
        hot[:, pl.ds(pl.multiple_of(j * LANES, LANES), LANES)] = one_hot_low(conn[pl.ds(j, 1), :])
        return carry

    lax.fori_loop(0, EB, body, 0, unroll=2)


def own_kernel(rows, conn, got):
    gather_own(rows, conn, got, (0, 1, 2))


def apply_kernel(
    freq, got_own, low, up, conn, hot, stiff, mass, got, terms, to_low, to_up, stack, total
):
    gather_ghosts(got_own, low, up, conn, got, (0, 1, 2))
    product(freq, got, stiff, mass, terms, 12, 2)
    scatter_blocks(terms, conn, hot, stack, total, 8, 12)
    for t in range(2):
        cols = slice(t * 256, (t + 1) * 256)
        to_low[:, cols] = total_tile(total, t)
        to_up[:, cols] = total_tile(total, 2 + t)


def sums_kernel(freq, terms, conn, hot, own, mass_row, p, stack, total):
    scatter_blocks(terms, conn, hot, stack, total, 0, 8)
    weights = edge_weights(freq, ROWS, 256)
    for t in range(8):
        cols = slice(t * 256, (t + 1) * 256)
        p[:, cols] = total_tile(total, t) + weights * mass_row[0:1, cols] * own[0:24, cols]


def finish_kernel(p, lists, from_low, from_up, own, to_low, to_up):
    arrived = jnp.concatenate([from_low[...], from_up[...]], axis=1)
    hots, stacks = [], []
    for c in range(2 * GHOST_T):
        index = lists[c // GHOST_T : c // GHOST_T + 1, (c % GHOST_T) * LANES : (c % GHOST_T + 1) * LANES]
        hots.append(one_hot_low(index))
        parts = pieces(arrived[:, c * LANES : (c + 1) * LANES])
        stacks.append(jnp.concatenate(masked_stack(parts, index, 0, 8), axis=0))
    sums = add_up(jnp.concatenate(stacks, axis=1), jnp.concatenate(hots, axis=1))
    for t in range(8):
        own[:, t * 256 : (t + 1) * 256] = p[:, t * 256 : (t + 1) * 256] + total_tile(sums, t)
    pick_listed(own, lists, (to_low, to_up), 3)


def quadratic(freq, got, got_rows, stiff, mass):
    result = jnp.zeros((8, LANES), f32)
    for h in range(2):
        weight = freq[h]
        for jt in range(8):

            def inner(i, sums):
                k = stiff[i, jt * 8 : jt * 8 + 8, :] + weight * mass[i, jt * 8 : jt * 8 + 8, :]
                return tuple(
                    s + k * jnp.broadcast_to(got[i, h * 12 + r : h * 12 + r + 1, :], (8, LANES))
                    for r, s in enumerate(sums)
                )

            zero = jnp.zeros((8, LANES), f32)
            sums = (zero,) * 12
            if jt < 7:
                sums = lax.fori_loop(jt * 8 + 8, EB, inner, sums, unroll=4)
                sums = tuple(s + s for s in sums)
            sums = lax.fori_loop(jt * 8, jt * 8 + 8, inner, sums, unroll=4)
            for r in range(12):
                mine = got_rows[pl.ds(jt * 8 * ROWS + h * 12 + r, 8, stride=ROWS), :]
                result = result + sums[r] * mine
    return result


def early_kernel(b_rows, w, moments):
    b = b_rows[0:24, :]
    moments[0:8, :] = fold(b * b)
    moments[8:16, :] = fold(b * w[...])
    moments[16:24, :] = fold(w[...] * w[...])


def third_kernel(
    freq, got_own, low, up, conn, stiff, mass, mass_row, w, v, early, got_rows, line_out, got
):
    gather_ghosts(got_own, low, up, conn, got, (0, 1, 2))
    for j in range(EB):
        got_rows[j * ROWS : (j + 1) * ROWS, :] = got[j]
    last = quadratic(freq, got, got_rows, stiff, mass)
    weights = edge_weights(freq, ROWS, 256)
    for t in range(8):
        cols = slice(t * 256, (t + 1) * 256)
        last = last + fold(weights * mass_row[0:1, cols] * v[:, cols] * v[:, cols])
    parts = [early[0:8, :], early[8:16, :], early[16:24, :], fold(w[...] * v[...]), fold(v[...] * v[...]), last]
    lane = lax.broadcasted_iota(i32, (1, LANES), 1)
    line = jnp.zeros((1, LANES), f32)
    for k, tile in enumerate(parts):
        line = line + jnp.where((lane & 7) == k, jnp.sum(tile), 0.0)
    line_out[...] = jnp.broadcast_to(line, (8, LANES))


def field_kernel(freq, rows, low, up, conn, stiff, mass, y, got_own, got):
    gather_own(rows, conn, got_own, (3,))
    gather_ghosts(got_own, low, up, conn, got, (3,))
    product(freq, got, stiff, mass, y, 2, 4)


def gradients(got_rows, y, node_block, node_shape, energy, out, base):
    for jt in range(8):
        ys = [y[r, jt * 8 : jt * 8 + 8, :] for r in range(4)]
        for o in range(6):
            term = jnp.zeros((8, LANES), f32)
            for h in range(2):
                for c in range(2):
                    x = got_rows[pl.ds(jt * 8 * ROWS + h * 12 + o * 2 + c, 8, stride=ROWS), :]
                    term = term - x * ys[h * 2 + c] if c else term + x * ys[h * 2 + c]
            energy[o, jt * 8 : jt * 8 + 8, :] = term

    def body(c, carry):
        index = jnp.broadcast_to(node_block[pl.ds(c, 1), :], (8, LANES))
        cols = pl.ds(pl.multiple_of(c * LANES, LANES), LANES)
        sums = [jnp.zeros((8, LANES), f32) for _ in range(18)]
        for jt in range(8):
            shape = [node_shape[k, jt * 8 : jt * 8 + 8, cols] for k in range(3)]
            for o in range(6):
                x = jnp.take_along_axis(energy[o, jt * 8 : jt * 8 + 8, :], index, axis=1, mode="promise_in_bounds")
                for k in range(3):
                    sums[o * 3 + k] = sums[o * 3 + k] - shape[k] * x
        for q in range(18):
            out[c, base + q : base + q + 1, :] = jnp.sum(sums[q], axis=0, keepdims=True)
        return carry

    lax.fori_loop(0, 8, body, 0)


def early_gradient_kernel(got0, got1, y, node_block, node_shape, out, energy):
    gradients(got0, y, node_block, node_shape, energy, out, 0)
    gradients(got1, y, node_block, node_shape, energy, out, 18)
    out[:, 36:40, :] = jnp.zeros((8, 4, LANES), f32)


def late_gradient_kernel(early, got2, y, node_block, node_shape, line, out, energy):
    out[:, 0:40, :] = early[...]
    gradients(got2, y, node_block, node_shape, energy, out, 40)
    for c in range(8):
        out[c, 58:64, :] = line[0:6, :]


def message_kernel(shares, out):
    line = shares[0, 60:61, :]
    for d in range(1, 8):
        line = line + shares[d, 60:61, :]
    out[...] = jnp.broadcast_to(line, (2, LANES))


def last_kernel(messages, rows, w, v, shares, adjoint, gradient):
    line = jnp.sum(messages[...], axis=0, keepdims=True)
    lane = lax.broadcasted_iota(i32, (1, LANES), 1)

    def moment(k):
        return jnp.sum(jnp.where((lane & 7) == k, line, 0.0), axis=1, keepdims=True)

    m = [moment(k) for k in range(6)]
    a0 = m[0] / m[1]
    r1 = (None, -a0)
    rr1 = m[0] - 2.0 * a0 * m[1] + a0 * a0 * m[2]
    b0 = rr1 / m[0]
    d1 = (1.0 + b0, -a0)
    dad1 = d1[0] * d1[0] * m[1] + 2.0 * d1[0] * d1[1] * m[2] + d1[1] * d1[1] * m[3]
    a1 = rr1 / dad1
    r2 = (None, r1[1] - a1 * d1[0], -a1 * d1[1])
    rr2 = (
        m[0] + 2.0 * r2[1] * m[1] + (2.0 * r2[2] + r2[1] * r2[1]) * m[2]
        + 2.0 * r2[1] * r2[2] * m[3] + r2[2] * r2[2] * m[4]
    )
    b1 = rr2 / rr1
    d2 = (1.0 + b1 * d1[0], r2[1] + b1 * d1[1], r2[2])
    dad2 = (
        d2[0] * d2[0] * m[1] + 2.0 * d2[0] * d2[1] * m[2] + (2.0 * d2[0] * d2[2] + d2[1] * d2[1]) * m[3]
        + 2.0 * d2[1] * d2[2] * m[4] + d2[2] * d2[2] * m[5]
    )
    a2 = rr2 / dad2
    c0 = a0 + a1 * d1[0] + a2 * d2[0]
    c1 = a1 * d1[1] + a2 * d2[1]
    c2 = a2 * d2[2]
    for h in range(2):
        for o in range(6):
            at = slice(h * 12 + o * 2, h * 12 + o * 2 + 2)
            adjoint[h, o] = c0 * rows[at, :] + c1 * w[at, :] + c2 * v[at, :]
    share = shares[0]
    for d in range(1, 8):
        share = share + shares[d]
    for o in range(6):
        gradient[o] = (
            c0 * share[o * 3 : o * 3 + 3] + c1 * share[18 + o * 3 : 21 + o * 3] + c2 * share[40 + o * 3 : 43 + o * 3]
        )


def shifted(x, by):
    count = lax.axis_size("mesh")
    return lax.ppermute(x, "mesh", [(i, i + by) for i in range(count) if 0 <= i + by < count])


def exchanged(to_low, to_up):
    return shifted(to_up, 1), shifted(to_low, -1)


def per_device(
    adjoint_rhs, forward_field, stiffness, mass_blocks, frequency, edge_mass, connectivity, send_list, node_block, node_shape
):
    lists = send_list[0]
    mass_row = edge_mass.reshape(1, EDGES)
    nodes = node_block.reshape(8, LANES)
    wide = CHUNK * LANES
    ghosts = (arr(ROWS, SLOTS), arr(ROWS, SLOTS))
    got_shape = arr(EB, ROWS, LANES)
    flat = lambda x: x.reshape(EB * ROWS, LANES)

    rows, to_low, to_up = kernel_call(
        prep_kernel, "prep", (arr(32, EDGES), arr(32, SLOTS), arr(32, SLOTS)), [VMEM] * 3,
        flops=10**6, nbytes=10**6,
    )(adjoint_rhs, forward_field, lists)
    rim_low, rim_up = exchanged(to_low, to_up)
    (hot,) = kernel_call(
        hot_kernel, "hot", (jax.ShapeDtypeStruct((256, EB * LANES), bf16),), [VMEM], flops=10**7, nbytes=4 * 10**6
    )(connectivity)

    def gathered_own(x):
        return kernel_call(own_kernel, "own", (got_shape,), [VMEM] * 2, flops=10**7, nbytes=10**7)(x, connectivity)[0]

    def applied(x, got_own, low, up):
        got, terms, to_low, to_up = kernel_call(
            apply_kernel, "apply", (got_shape, arr(ROWS, EB, LANES)) + ghosts, [SMEM] + [VMEM] * 7,
            [pltpu.VMEM((4 * 48, wide), bf16), pltpu.VMEM((4 * 48, 256), f32)],
            flops=10**8, nbytes=10**7,
        )(frequency, got_own, low, up, connectivity, hot, stiffness, mass_blocks)
        from_low, from_up = exchanged(to_low, to_up)
        (p,) = kernel_call(
            sums_kernel, "sums", (arr(ROWS, EDGES),), [SMEM] + [VMEM] * 5,
            [pltpu.VMEM((8 * 48, wide), bf16), pltpu.VMEM((8 * 48, 256), f32)], flops=10**8, nbytes=10**7,
        )(frequency, terms, connectivity, hot, x, mass_row)
        own, to_low, to_up = kernel_call(
            finish_kernel, "finish", (arr(ROWS, EDGES),) + ghosts, [VMEM] * 4, flops=10**7, nbytes=10**6
        )(p, lists, from_low, from_up)
        return got, own, exchanged(to_low, to_up)

    got0, w, (low, up) = applied(rows, gathered_own(rows), rim_low, rim_up)
    w_own = gathered_own(w)
    (y,) = kernel_call(
        field_kernel, "field", (arr(4, EB, LANES),), [SMEM] + [VMEM] * 6,
        [pltpu.VMEM((EB, 8, LANES), f32), pltpu.VMEM((EB, 8, LANES), f32)],
        flops=10**8, nbytes=10**7,
    )(frequency, rows, rim_low, rim_up, connectivity, stiffness, mass_blocks)
    got1, v, (low, up) = applied(w, w_own, low, up)
    v_own = gathered_own(v)
    (early,) = kernel_call(early_kernel, "early", (arr(24, LANES),), [VMEM] * 2, flops=10**6, nbytes=10**6)(rows, w)
    (grads,) = kernel_call(
        early_gradient_kernel, "early_gradient", (arr(8, 40, LANES),), [VMEM] * 5, [pltpu.VMEM((6, EB, LANES), f32)],
        flops=10**8, nbytes=10**7,
    )(flat(got0), flat(got1), y, nodes, node_shape)
    got2, line = kernel_call(
        third_kernel, "third", (arr(EB * ROWS, LANES), arr(8, LANES)), [SMEM] + [VMEM] * 10,
        [pltpu.VMEM((EB, ROWS, LANES), f32)], flops=10**8, nbytes=10**7,
    )(frequency, v_own, low, up, connectivity, stiffness, mass_blocks, mass_row, w, v, early)
    (grads,) = kernel_call(
        late_gradient_kernel, "late_gradient", (arr(8, 64, LANES),), [VMEM] * 6, [pltpu.VMEM((6, EB, LANES), f32)],
        flops=10**8, nbytes=10**7,
    )(grads, got2, y, nodes, node_shape, line)
    shares = lax.all_to_all(grads, "harm", 0, 0, tiled=True)
    (message,) = kernel_call(message_kernel, "message", (arr(2, LANES),), [VMEM], flops=10**3, nbytes=10**5)(shares)
    messages = lax.all_to_all(message.reshape(2 * LANES), "mesh", 0, 0, tiled=True).reshape(2, LANES)
    adjoint, gradient = kernel_call(
        last_kernel, "last", (arr(*adjoint_rhs.shape), arr(6, 3, LANES)), [VMEM] * 5, flops=10**6, nbytes=10**6
    )(messages, rows, w, v, shares)
    return adjoint, gradient


def solution(mesh):
    return jax.shard_map(
        per_device,
        mesh=mesh,
        in_specs=(
            P("harm", None, None, "mesh"),
            P("harm", None, "mesh"),
            P(None, None, "mesh"),
            P(None, None, "mesh"),
            P("harm"),
            P("mesh"),
            P(None, "mesh"),
            P("mesh", None, None),
            P("mesh"),
            P(None, None, "mesh"),
        ),
        out_specs=(P("harm", None, None, "mesh"), P(None, None, ("mesh", "harm"))),
        check_vma=False,
    )
```

```python
import functools

import jax
import jax.numpy as jnp
from jax import lax
from jax.experimental import pallas as pl
from jax.experimental.pallas import tpu as pltpu
from jax.sharding import PartitionSpec as P

f32 = jnp.float32
bf16 = jnp.bfloat16
i32 = jnp.int32
LANES = 128
EDGES = 2048
SLOTS = 512
ROWS = 24
EB = 64
OWN_T, GHOST_T = EDGES // LANES, SLOTS // LANES
BOTH = ("mesh", "harm")

VMEM = pl.BlockSpec(memory_space=pltpu.VMEM)
SMEM = pl.BlockSpec(memory_space=pltpu.SMEM)


def kernel_call(body, name, out, specs, scratch=(), flops=0, nbytes=0):
    return pl.pallas_call(
        body,
        name=name,
        out_shape=out,
        in_specs=specs,
        out_specs=jax.tree.map(lambda _: VMEM, out),
        scratch_shapes=scratch,
        compiler_params=pltpu.CompilerParams(vmem_limit_bytes=20 * 2**20),
        cost_estimate=pl.CostEstimate(flops=flops, bytes_accessed=nbytes, transcendentals=0),
    )


def arr(*shape):
    return jax.ShapeDtypeStruct(shape, f32)


def lookup(tables, index):
    lane = jnp.broadcast_to(index & (LANES - 1), (8, LANES))
    high = jnp.broadcast_to(index >> 7, (8, LANES))
    found = [jnp.take_along_axis(t, lane, axis=1, mode="promise_in_bounds") for t in tables]
    bit = 1
    while len(found) > 1:
        odd = (high & bit) != 0
        found = [
            jnp.where(odd, found[a + 1], found[a]) if a + 1 < len(found) else found[a]
            for a in range(0, len(found), 2)
        ]
        bit *= 2
    return found[0]


def tiles(ref, row, count):
    return [ref[row : row + 8, t * LANES : (t + 1) * LANES] for t in range(count)]


WIDE = 512
PARTS = (EDGES + 2 * SLOTS) // WIDE
CHUNK = 16


def gather_blocks(own, low, up, conn, hot, stack, outs):
    count = own.shape[0]
    for t in range(PARTS):
        x = own[:, t * WIDE : (t + 1) * WIDE] if t < PARTS - 2 else (low if t == PARTS - 2 else up)[...]
        stack[t * 2 * count : (t + 1) * 2 * count, :] = pieces(x)

    def body(c, carry):
        cols = pl.ds(pl.multiple_of(c * CHUNK * LANES, CHUNK * LANES), CHUNK * LANES)
        found = jnp.dot(stack[...], hot[:, cols], preferred_element_type=f32)
        for jj in range(CHUNK):
            j = c * CHUNK + jj
            high = conn[pl.ds(j, 1), :] >> 9
            for out, first, rows in outs:
                value = None
                for t in range(PARTS):
                    at = t * 2 * count + first
                    lanes = slice(jj * LANES, (jj + 1) * LANES)
                    x = found[at : at + rows, lanes] + found[at + count : at + count + rows, lanes]
                    value = x if t == 0 else jnp.where(jnp.broadcast_to(high, x.shape) == t, x, value)
                out[pl.ds(pl.multiple_of(j * rows, 8), rows), :] = value
        return carry

    lax.fori_loop(0, EB // CHUNK, body, 0)


def product(blocks, got, out, per_harm, per_edge, wide):
    for h in range(2):

        def outer(jt, carry):
            def inner(i, sums):
                ks = []
                for q in range(wide):
                    rows = pl.ds(pl.multiple_of((jt * wide + q) * 8, 8), 8)
                    ks.append(blocks[h, i, rows, :])
                new = []
                for r in range(per_harm):
                    x = jnp.broadcast_to(got[pl.ds(i * per_edge + h * per_harm + r, 1), :], (8, LANES))
                    for q in range(wide):
                        new.append(sums[r * wide + q] + ks[q] * x)
                return tuple(new)

            zero = jnp.zeros((8, LANES), f32)
            sums = lax.fori_loop(0, EB, inner, (zero,) * (per_harm * wide), unroll=8)
            for r in range(per_harm):
                for q in range(wide):
                    at = (h * per_harm + r) * EB + (jt * wide + q) * 8
                    out[pl.ds(pl.multiple_of(at, 8), 8), :] = sums[r * wide + q]
            return carry

        lax.fori_loop(0, EB // (8 * wide), outer, 0)


def pieces(x):
    high = x.astype(bf16).astype(f32)
    return jnp.concatenate([high, x - high], axis=0).astype(bf16)


def one_hot_low(index):
    low = jnp.broadcast_to(index & 255, (256, LANES))
    return jnp.where(low == lax.broadcasted_iota(i32, (256, LANES), 0), 1.0, 0.0).astype(bf16)


def masked_stack(parts, index, first, last):
    high = index >> 8
    stack = []
    for t in range(first, last):
        mask = jnp.broadcast_to(jnp.where(high == t, 1.0, 0.0), parts.shape).astype(bf16)
        stack.append(parts * mask)
    return stack


def add_up(stack, hot):
    return lax.dot_general(stack, hot, (((1,), (1,)), ((), ())), preferred_element_type=f32)


def scatter_blocks(terms, conn, hot, stack, total):
    total[...] = jnp.zeros_like(total)
    for c in range(EB // CHUNK):

        def body(jj, carry):
            j = c * CHUNK + jj
            cols = pl.ds(pl.multiple_of(jj * LANES, LANES), LANES)
            x = terms[pl.ds(j, ROWS, stride=EB), :]
            first = x.astype(bf16).astype(f32)
            rest = x - first
            high = jnp.broadcast_to(conn[pl.ds(j, 1), :] >> 9, (ROWS, LANES))
            for t in range(PARTS):
                here = high == t
                both = jnp.concatenate([jnp.where(here, first, 0.0), jnp.where(here, rest, 0.0)], axis=0)
                stack[t * 48 : t * 48 + 48, cols] = both.astype(bf16)
            return carry

        lax.fori_loop(0, CHUNK, body, 0, unroll=CHUNK)
        total[...] += add_up(stack[...], hot[:, c * CHUNK * LANES : (c + 1) * CHUNK * LANES])


def total_tile(total, t):
    return total[t * 48 : t * 48 + 24, :] + total[t * 48 + 24 : t * 48 + 48, :]


def edge_weights(freq, rows, width):
    upper = lax.broadcasted_iota(i32, (rows, width), 0) < rows // 2
    return jnp.where(upper, freq[0], freq[1])


def pick_listed(source, lists, outs, groups):
    for side in range(2):
        for c in range(GHOST_T):
            cols = slice(c * LANES, (c + 1) * LANES)
            index = lists[side : side + 1, cols]
            for g in range(groups):
                value = lookup(tiles(source, g * 8, OWN_T), index)
                outs[side][g * 8 : g * 8 + 8, cols] = jnp.where(index >= 0, value, 0.0)


def fold(x):
    rows, cols = x.shape
    total = jnp.zeros((8, LANES), f32)
    for r in range(rows // 8):
        for c in range(cols // LANES):
            total = total + x[r * 8 : r * 8 + 8, c * LANES : (c + 1) * LANES]
    return total


def prep_kernel(rhs, field, lists, rows, to_low, to_up):
    for h in range(2):
        for o in range(6):
            at = h * 12 + o * 2
            rows[at : at + 2, :] = rhs[h, o]
        rows[24 + 2 * h : 26 + 2 * h, :] = field[h]
    rows[28:32, :] = jnp.zeros((4, EDGES), f32)
    pick_listed(rows, lists, (to_low, to_up), 4)


def hot_kernel(conn, hot):
    def body(j, carry):
        low = jnp.broadcast_to(conn[pl.ds(j, 1), :] & (WIDE - 1), (WIDE, LANES))
        one = jnp.where(low == lax.broadcasted_iota(i32, (WIDE, LANES), 0), 1.0, 0.0).astype(bf16)
        hot[:, pl.ds(pl.multiple_of(j * LANES, LANES), LANES)] = one
        return carry

    lax.fori_loop(0, EB, body, 0, unroll=4)


def blocks_kernel(freq, stiff, mass, blocks):
    def body(i, carry):
        for h in range(2):
            blocks[h, i] = stiff[i] + freq[h] * mass[i]
        return carry

    lax.fori_loop(0, EB, body, 0, unroll=2)


def apply_kernel(with_field, freq, own, low, up, conn, hot, blocks, mass_row, p, to_low, to_up, got, *refs):
    stack, terms, masked, total = refs[-4:]
    outs = [(got, 0, ROWS)] + ([(refs[0], ROWS, 8)] if with_field else [])
    gather_blocks(own, low, up, conn, hot, stack, outs)
    product(blocks, got, terms, 12, ROWS, 2)
    scatter_blocks(terms, conn, hot, masked, total)
    weights = edge_weights(freq, ROWS, WIDE)
    for t in range(PARTS):
        sums = total[t * 48 : t * 48 + 24, :] + total[t * 48 + 24 : t * 48 + 48, :]
        if t < PARTS - 2:
            cols = slice(t * WIDE, (t + 1) * WIDE)
            p[:, cols] = sums + weights * mass_row[0:1, cols] * own[0:ROWS, cols]
        else:
            (to_low if t == PARTS - 2 else to_up)[...] = sums


def finish_kernel(p, lists, from_low, from_up, own, to_low, to_up):
    arrived = jnp.concatenate([from_low[...], from_up[...]], axis=1)
    hots, stacks = [], []
    for c in range(2 * GHOST_T):
        index = lists[c // GHOST_T : c // GHOST_T + 1, (c % GHOST_T) * LANES : (c % GHOST_T + 1) * LANES]
        hots.append(one_hot_low(index))
        parts = pieces(arrived[:, c * LANES : (c + 1) * LANES])
        stacks.append(jnp.concatenate(masked_stack(parts, index, 0, 8), axis=0))
    sums = add_up(jnp.concatenate(stacks, axis=1), jnp.concatenate(hots, axis=1))
    for t in range(8):
        own[:, t * 256 : (t + 1) * 256] = p[:, t * 256 : (t + 1) * 256] + total_tile(sums, t)
    pick_listed(own, lists, (to_low, to_up), 3)


def quadratic(blocks, got):
    result = jnp.zeros((8, LANES), f32)
    for h in range(2):
        for jt in range(8):

            def inner(i, sums):
                k = blocks[h, i, jt * 8 : jt * 8 + 8, :]
                return tuple(
                    s + k * jnp.broadcast_to(got[pl.ds(i * ROWS + h * 12 + r, 1), :], (8, LANES))
                    for r, s in enumerate(sums)
                )

            zero = jnp.zeros((8, LANES), f32)
            sums = (zero,) * 12
            if jt < 7:
                sums = lax.fori_loop(jt * 8 + 8, EB, inner, sums, unroll=4)
                sums = tuple(s + s for s in sums)
            sums = lax.fori_loop(jt * 8, jt * 8 + 8, inner, sums, unroll=4)
            for r in range(12):
                mine = got[pl.ds(jt * 8 * ROWS + h * 12 + r, 8, stride=ROWS), :]
                result = result + sums[r] * mine
    return result


def early_kernel(b_rows, w, moments):
    b = b_rows[0:24, :]
    moments[0:8, :] = fold(b * b)
    moments[8:16, :] = fold(b * w[...])
    moments[16:24, :] = fold(w[...] * w[...])


def third_kernel(freq, v, low, up, conn, hot, blocks, mass_row, w, early, got, line_out, stack):
    gather_blocks(v, low, up, conn, hot, stack, [(got, 0, ROWS)])
    last = quadratic(blocks, got)
    weights = edge_weights(freq, ROWS, 256)
    for t in range(8):
        cols = slice(t * 256, (t + 1) * 256)
        last = last + fold(weights * mass_row[0:1, cols] * v[:, cols] * v[:, cols])
    parts = [early[0:8, :], early[8:16, :], early[16:24, :], fold(w[...] * v[...]), fold(v[...] * v[...]), last]
    lane = lax.broadcasted_iota(i32, (1, LANES), 1)
    line = jnp.zeros((1, LANES), f32)
    for k, tile in enumerate(parts):
        line = line + jnp.where((lane & 7) == k, jnp.sum(tile), 0.0)
    line_out[...] = jnp.broadcast_to(line, (8, LANES))


def field_kernel(blocks, got, y):
    product(blocks, got, y, 2, 8, 4)


def gradients(got_rows, y, node_block, node_shape, energy, out, base):
    for jt in range(8):
        ys = [y[r * EB + jt * 8 : r * EB + jt * 8 + 8, :] for r in range(4)]
        for o in range(6):
            term = jnp.zeros((8, LANES), f32)
            for h in range(2):
                for c in range(2):
                    x = got_rows[pl.ds(jt * 8 * ROWS + h * 12 + o * 2 + c, 8, stride=ROWS), :]
                    term = term - x * ys[h * 2 + c] if c else term + x * ys[h * 2 + c]
            energy[o, jt * 8 : jt * 8 + 8, :] = term

    def body(c, carry):
        index = jnp.broadcast_to(node_block[pl.ds(c, 1), :], (8, LANES))
        cols = pl.ds(pl.multiple_of(c * LANES, LANES), LANES)
        sums = [jnp.zeros((8, LANES), f32) for _ in range(18)]
        for jt in range(8):
            shape = [node_shape[k, jt * 8 : jt * 8 + 8, cols] for k in range(3)]
            for o in range(6):
                x = jnp.take_along_axis(energy[o, jt * 8 : jt * 8 + 8, :], index, axis=1, mode="promise_in_bounds")
                for k in range(3):
                    sums[o * 3 + k] = sums[o * 3 + k] - shape[k] * x
        for q in range(18):
            out[c, base + q : base + q + 1, :] = jnp.sum(sums[q], axis=0, keepdims=True)
        return carry

    lax.fori_loop(0, 8, body, 0)


def early_gradient_kernel(got0, got1, y, node_block, node_shape, out, energy):
    gradients(got0, y, node_block, node_shape, energy, out, 0)
    gradients(got1, y, node_block, node_shape, energy, out, 18)
    out[:, 36:40, :] = jnp.zeros((8, 4, LANES), f32)


def late_gradient_kernel(early, got2, y, node_block, node_shape, line, out, energy):
    out[:, 0:40, :] = early[...]
    gradients(got2, y, node_block, node_shape, energy, out, 40)
    for c in range(8):
        out[c, 58:64, :] = line[0:6, :]


def message_kernel(shares, out):
    line = shares[0, 60:61, :]
    for d in range(1, 8):
        line = line + shares[d, 60:61, :]
    out[...] = jnp.broadcast_to(line, (32, LANES))


def last_kernel(messages, rows, w, v, shares, adjoint, gradient):
    line = jnp.sum(messages[...], axis=0, keepdims=True)
    lane = lax.broadcasted_iota(i32, (1, LANES), 1)

    def moment(k):
        return jnp.sum(jnp.where((lane & 7) == k, line, 0.0), axis=1, keepdims=True)

    m = [moment(k) for k in range(6)]
    a0 = m[0] / m[1]
    r1 = (None, -a0)
    rr1 = m[0] - 2.0 * a0 * m[1] + a0 * a0 * m[2]
    b0 = rr1 / m[0]
    d1 = (1.0 + b0, -a0)
    dad1 = d1[0] * d1[0] * m[1] + 2.0 * d1[0] * d1[1] * m[2] + d1[1] * d1[1] * m[3]
    a1 = rr1 / dad1
    r2 = (None, r1[1] - a1 * d1[0], -a1 * d1[1])
    rr2 = (
        m[0] + 2.0 * r2[1] * m[1] + (2.0 * r2[2] + r2[1] * r2[1]) * m[2]
        + 2.0 * r2[1] * r2[2] * m[3] + r2[2] * r2[2] * m[4]
    )
    b1 = rr2 / rr1
    d2 = (1.0 + b1 * d1[0], r2[1] + b1 * d1[1], r2[2])
    dad2 = (
        d2[0] * d2[0] * m[1] + 2.0 * d2[0] * d2[1] * m[2] + (2.0 * d2[0] * d2[2] + d2[1] * d2[1]) * m[3]
        + 2.0 * d2[1] * d2[2] * m[4] + d2[2] * d2[2] * m[5]
    )
    a2 = rr2 / dad2
    c0 = a0 + a1 * d1[0] + a2 * d2[0]
    c1 = a1 * d1[1] + a2 * d2[1]
    c2 = a2 * d2[2]
    for h in range(2):
        for o in range(6):
            at = slice(h * 12 + o * 2, h * 12 + o * 2 + 2)
            adjoint[h, o] = c0 * rows[at, :] + c1 * w[at, :] + c2 * v[at, :]
    share = shares[0]
    for d in range(1, 8):
        share = share + shares[d]
    for o in range(6):
        gradient[o] = (
            c0 * share[o * 3 : o * 3 + 3] + c1 * share[18 + o * 3 : 21 + o * 3] + c2 * share[40 + o * 3 : 43 + o * 3]
        )


def shifted(x, by):
    count = lax.axis_size("mesh")
    return lax.ppermute(x, "mesh", [(i, i + by) for i in range(count) if 0 <= i + by < count])


def exchanged(to_low, to_up):
    return shifted(to_up, 1), shifted(to_low, -1)


def per_device(
    adjoint_rhs, forward_field, stiffness, mass_blocks, frequency, edge_mass, connectivity, send_list, node_block, node_shape
):
    lists = send_list[0]
    mass_row = edge_mass.reshape(1, EDGES)
    nodes = node_block.reshape(8, LANES)
    ghosts = (arr(ROWS, SLOTS), arr(ROWS, SLOTS))
    got_shape = arr(EB * ROWS, LANES)
    medium = dict(flops=10**9, nbytes=10**7)

    rows, to_low, to_up = kernel_call(
        prep_kernel, "prep", (arr(32, EDGES), arr(32, SLOTS), arr(32, SLOTS)), [VMEM] * 3, flops=10**6, nbytes=10**6
    )(adjoint_rhs, forward_field, lists)
    low, up = exchanged(to_low, to_up)
    (hot,) = kernel_call(
        hot_kernel, "hot", (jax.ShapeDtypeStruct((WIDE, EB * LANES), bf16),), [VMEM], **medium
    )(connectivity)
    (blocks,) = kernel_call(blocks_kernel, "blocks", (arr(2, EB, EB, LANES),), [SMEM] + [VMEM] * 2, **medium)(
        frequency, stiffness, mass_blocks
    )

    def applied(x, low, up, with_field):
        count = 2 * PARTS * x.shape[0]
        p, to_low, to_up, *got = kernel_call(
            functools.partial(apply_kernel, with_field), "apply",
            (arr(ROWS, EDGES),) + ghosts + (got_shape,) + (arr(EB * 8, LANES),) * with_field, [SMEM] + [VMEM] * 7,
            [
                pltpu.VMEM((count, WIDE), bf16),
                pltpu.VMEM((ROWS * EB, LANES), f32),
                pltpu.VMEM((PARTS * 48, CHUNK * LANES), bf16),
                pltpu.VMEM((PARTS * 48, WIDE), f32),
            ],
            **medium,
        )(frequency, x, low, up, connectivity, hot, blocks, mass_row)
        from_low, from_up = exchanged(to_low, to_up)
        own, to_low, to_up = kernel_call(
            finish_kernel, "finish", (arr(ROWS, EDGES),) + ghosts, [VMEM] * 4, flops=10**7, nbytes=10**6
        )(p, lists, from_low, from_up)
        return got, own, exchanged(to_low, to_up)

    (got0, got_field), w, (low, up) = applied(rows, low, up, True)
    (y,) = kernel_call(field_kernel, "field", (arr(4 * EB, LANES),), [VMEM] * 2, **medium)(blocks, got_field)
    (got1,), v, (low, up) = applied(w, low, up, False)
    (grads,) = kernel_call(
        early_gradient_kernel, "early_gradient", (arr(8, 40, LANES),), [VMEM] * 5, [pltpu.VMEM((6, EB, LANES), f32)], **medium
    )(got0, got1, y, nodes, node_shape)
    (early,) = kernel_call(early_kernel, "early", (arr(24, LANES),), [VMEM] * 2, flops=10**6, nbytes=10**6)(rows, w)
    got2, line = kernel_call(
        third_kernel, "third", (got_shape, arr(8, LANES)), [SMEM] + [VMEM] * 9,
        [pltpu.VMEM((PARTS * 48, WIDE), bf16)], **medium,
    )(frequency, v, low, up, connectivity, hot, blocks, mass_row, w, early)
    (grads,) = kernel_call(
        late_gradient_kernel, "late_gradient", (arr(8, 64, LANES),), [VMEM] * 6, [pltpu.VMEM((6, EB, LANES), f32)], **medium
    )(grads, got2, y, nodes, node_shape, line)
    shares = lax.all_to_all(grads, "harm", 0, 0, tiled=True)
    (message,) = kernel_call(message_kernel, "message", (arr(32, LANES),), [VMEM], flops=10**3, nbytes=10**5)(shares)
    messages = lax.all_to_all(message.reshape(32 * LANES), "mesh", 0, 0, tiled=True).reshape(32, LANES)
    adjoint, gradient = kernel_call(
        last_kernel, "last", (arr(*adjoint_rhs.shape), arr(6, 3, LANES)), [VMEM] * 5, flops=10**6, nbytes=10**6
    )(messages, rows, w, v, shares)
    return adjoint, gradient


def solution(mesh):
    return jax.shard_map(
        per_device,
        mesh=mesh,
        in_specs=(
            P("harm", None, None, "mesh"),
            P("harm", None, "mesh"),
            P(None, None, "mesh"),
            P(None, None, "mesh"),
            P("harm"),
            P("mesh"),
            P(None, "mesh"),
            P("mesh", None, None),
            P("mesh"),
            P(None, None, "mesh"),
        ),
        out_specs=(P("harm", None, None, "mesh"), P(None, None, ("mesh", "harm"))),
        check_vma=False,
    )
```

```python
import functools

import jax
import jax.numpy as jnp
from jax import lax
from jax.experimental import pallas as pl
from jax.experimental.pallas import tpu as pltpu
from jax.sharding import PartitionSpec as P

f32 = jnp.float32
bf16 = jnp.bfloat16
i32 = jnp.int32
LANES = 128
EDGES = 2048
SLOTS = 512
ROWS = 24
EB = 64
OWN_T, GHOST_T = EDGES // LANES, SLOTS // LANES
BOTH = ("mesh", "harm")

VMEM = pl.BlockSpec(memory_space=pltpu.VMEM)
SMEM = pl.BlockSpec(memory_space=pltpu.SMEM)
HBM = pl.BlockSpec(memory_space=pltpu.HBM)


def kernel_call(body, name, out, specs, scratch=(), flops=0, nbytes=0, limit=20):
    return pl.pallas_call(
        body,
        name=name,
        out_shape=out,
        in_specs=specs,
        out_specs=jax.tree.map(lambda _: VMEM, out),
        scratch_shapes=scratch,
        compiler_params=pltpu.CompilerParams(vmem_limit_bytes=limit * 2**20),
        cost_estimate=pl.CostEstimate(flops=flops, bytes_accessed=nbytes, transcendentals=0),
    )


def arr(*shape):
    return jax.ShapeDtypeStruct(shape, f32)


def lookup(tables, index):
    lane = jnp.broadcast_to(index & (LANES - 1), (8, LANES))
    high = jnp.broadcast_to(index >> 7, (8, LANES))
    found = [jnp.take_along_axis(t, lane, axis=1, mode="promise_in_bounds") for t in tables]
    bit = 1
    while len(found) > 1:
        odd = (high & bit) != 0
        found = [
            jnp.where(odd, found[a + 1], found[a]) if a + 1 < len(found) else found[a]
            for a in range(0, len(found), 2)
        ]
        bit *= 2
    return found[0]


def tiles(ref, row, count):
    return [ref[row : row + 8, t * LANES : (t + 1) * LANES] for t in range(count)]


WIDE = 512
PARTS = (EDGES + 2 * SLOTS) // WIDE
CHUNK = 16


def gather_blocks(own, low, up, conn, hot, stack, outs):
    count = own.shape[0]
    for t in range(PARTS):
        x = own[:, t * WIDE : (t + 1) * WIDE] if t < PARTS - 2 else (low if t == PARTS - 2 else up)[...]
        stack[t * 2 * count : (t + 1) * 2 * count, :] = pieces(x)

    def body(c, carry):
        cols = pl.ds(pl.multiple_of(c * CHUNK * LANES, CHUNK * LANES), CHUNK * LANES)
        found = jnp.dot(stack[...], hot[:, cols], preferred_element_type=f32)
        for jj in range(CHUNK):
            j = c * CHUNK + jj
            high = conn[pl.ds(j, 1), :] >> 9
            for out, first, rows in outs:
                value = None
                for t in range(PARTS):
                    at = t * 2 * count + first
                    lanes = slice(jj * LANES, (jj + 1) * LANES)
                    x = found[at : at + rows, lanes] + found[at + count : at + count + rows, lanes]
                    value = x if t == 0 else jnp.where(jnp.broadcast_to(high, x.shape) == t, x, value)
                out[pl.ds(pl.multiple_of(j * rows, 8), rows), :] = value
        return carry

    lax.fori_loop(0, EB // CHUNK, body, 0)


def product(blocks, got, out, per_harm, per_edge, wide):
    for h in range(2):

        def outer(jt, carry):
            def inner(i, sums):
                ks = []
                for q in range(wide):
                    rows = pl.ds(pl.multiple_of((jt * wide + q) * 8, 8), 8)
                    ks.append(blocks[h, i, rows, :])
                new = []
                for r in range(per_harm):
                    x = jnp.broadcast_to(got[pl.ds(i * per_edge + h * per_harm + r, 1), :], (8, LANES))
                    for q in range(wide):
                        new.append(sums[r * wide + q] + ks[q] * x)
                return tuple(new)

            zero = jnp.zeros((8, LANES), f32)
            sums = lax.fori_loop(0, EB, inner, (zero,) * (per_harm * wide), unroll=8)
            for r in range(per_harm):
                for q in range(wide):
                    at = (h * per_harm + r) * EB + (jt * wide + q) * 8
                    out[pl.ds(pl.multiple_of(at, 8), 8), :] = sums[r * wide + q]
            return carry

        lax.fori_loop(0, EB // (8 * wide), outer, 0)


def pieces(x):
    high = x.astype(bf16).astype(f32)
    return jnp.concatenate([high, x - high], axis=0).astype(bf16)


def one_hot_low(index):
    low = jnp.broadcast_to(index & 255, (256, LANES))
    return jnp.where(low == lax.broadcasted_iota(i32, (256, LANES), 0), 1.0, 0.0).astype(bf16)


def masked_stack(parts, index, first, last):
    high = index >> 8
    stack = []
    for t in range(first, last):
        mask = jnp.broadcast_to(jnp.where(high == t, 1.0, 0.0), parts.shape).astype(bf16)
        stack.append(parts * mask)
    return stack


def add_up(stack, hot):
    return lax.dot_general(stack, hot, (((1,), (1,)), ((), ())), preferred_element_type=f32)


def scatter_blocks(terms, conn, hot, stack, total, first, last):
    total[...] = jnp.zeros_like(total)
    for c in range(EB // CHUNK):

        def body(jj, carry):
            j = c * CHUNK + jj
            cols = pl.ds(pl.multiple_of(jj * LANES, LANES), LANES)
            x = terms[pl.ds(j, ROWS, stride=EB), :]
            head = x.astype(bf16).astype(f32)
            rest = x - head
            high = jnp.broadcast_to(conn[pl.ds(j, 1), :] >> 9, (ROWS, LANES))
            for t in range(first, last):
                here = high == t
                both = jnp.concatenate([jnp.where(here, head, 0.0), jnp.where(here, rest, 0.0)], axis=0)
                at = (t - first) * 48
                stack[at : at + 48, cols] = both.astype(bf16)
            return carry

        lax.fori_loop(0, CHUNK, body, 0, unroll=CHUNK)
        total[...] += add_up(stack[...], hot[:, c * CHUNK * LANES : (c + 1) * CHUNK * LANES])


def total_tile(total, t):
    return total[t * 48 : t * 48 + 24, :] + total[t * 48 + 24 : t * 48 + 48, :]


def edge_weights(freq, rows, width):
    upper = lax.broadcasted_iota(i32, (rows, width), 0) < rows // 2
    return jnp.where(upper, freq[0], freq[1])


def pick_listed(source, lists, outs, groups):
    for side in range(2):
        for c in range(GHOST_T):
            cols = slice(c * LANES, (c + 1) * LANES)
            index = lists[side : side + 1, cols]
            for g in range(groups):
                value = lookup(tiles(source, g * 8, OWN_T), index)
                outs[side][g * 8 : g * 8 + 8, cols] = jnp.where(index >= 0, value, 0.0)


def fold(x):
    rows, cols = x.shape
    total = jnp.zeros((8, LANES), f32)
    for r in range(rows // 8):
        for c in range(cols // LANES):
            total = total + x[r * 8 : r * 8 + 8, c * LANES : (c + 1) * LANES]
    return total


def prep_kernel(rhs_in, field_in, lists_in, rows, to_low, to_up, rhs, field, lists, sems):
    copies = [
        pltpu.make_async_copy(a, b, sems.at[k])
        for k, (a, b) in enumerate(((rhs_in, rhs), (field_in, field), (lists_in, lists)))
    ]
    for copy in copies:
        copy.start()
    for copy in copies:
        copy.wait()
    for h in range(2):
        for o in range(6):
            at = h * 12 + o * 2
            rows[at : at + 2, :] = rhs[h, o]
        rows[24 + 2 * h : 26 + 2 * h, :] = field[h]
    rows[28:32, :] = jnp.zeros((4, EDGES), f32)
    pick_listed(rows, lists, (to_low, to_up), 4)


def hot_kernel(conn, hot):
    def body(j, carry):
        low = jnp.broadcast_to(conn[pl.ds(j, 1), :] & (WIDE - 1), (WIDE, LANES))
        one = jnp.where(low == lax.broadcasted_iota(i32, (WIDE, LANES), 0), 1.0, 0.0)
        cols = pl.ds(pl.multiple_of(j * LANES, LANES), LANES)
        hot[:, cols] = one.astype(bf16)
        return carry

    lax.fori_loop(0, EB, body, 0, unroll=4)


def blocks_kernel(freq, stiff, mass, blocks):
    def body(i, carry):
        for h in range(2):
            blocks[h, i] = stiff[i] + freq[h] * mass[i]
        return carry

    lax.fori_loop(0, EB, body, 0, unroll=2)


def apply_kernel(with_field, own, low, up, conn, hot, blocks, terms, to_low, to_up, got, *refs):
    stack, masked, total = refs[-3:]
    outs = [(got, 0, ROWS)] + ([(refs[0], ROWS, 8)] if with_field else [])
    gather_blocks(own, low, up, conn, hot, stack, outs)
    product(blocks, got, terms, 12, ROWS, 2)
    scatter_blocks(terms, conn, hot, masked, total, 4, 6)
    to_low[...] = total_tile(total, 0)
    to_up[...] = total_tile(total, 1)


def sums_kernel(freq, terms, conn, hot, own, mass_row, p, masked, total):
    scatter_blocks(terms, conn, hot, masked, total, 0, 4)
    weights = edge_weights(freq, ROWS, WIDE)
    for t in range(4):
        cols = slice(t * WIDE, (t + 1) * WIDE)
        p[:, cols] = total_tile(total, t) + weights * mass_row[0:1, cols] * own[0:ROWS, cols]


def finish_kernel(p, lists, from_low, from_up, own, to_low, to_up):
    arrived = jnp.concatenate([from_low[...], from_up[...]], axis=1)
    hots, stacks = [], []
    for c in range(2 * GHOST_T):
        index = lists[c // GHOST_T : c // GHOST_T + 1, (c % GHOST_T) * LANES : (c % GHOST_T + 1) * LANES]
        hots.append(one_hot_low(index))
        parts = pieces(arrived[:, c * LANES : (c + 1) * LANES])
        stacks.append(jnp.concatenate(masked_stack(parts, index, 0, 8), axis=0))
    sums = add_up(jnp.concatenate(stacks, axis=1), jnp.concatenate(hots, axis=1))
    for t in range(8):
        own[:, t * 256 : (t + 1) * 256] = p[:, t * 256 : (t + 1) * 256] + total_tile(sums, t)
    pick_listed(own, lists, (to_low, to_up), 3)


def quadratic(blocks, got):
    result = jnp.zeros((8, LANES), f32)
    for h in range(2):
        for jt in range(8):

            def inner(i, sums):
                k = blocks[h, i, jt * 8 : jt * 8 + 8, :]
                return tuple(
                    s + k * jnp.broadcast_to(got[pl.ds(i * ROWS + h * 12 + r, 1), :], (8, LANES))
                    for r, s in enumerate(sums)
                )

            zero = jnp.zeros((8, LANES), f32)
            sums = (zero,) * 12
            if jt < 7:
                sums = lax.fori_loop(jt * 8 + 8, EB, inner, sums, unroll=4)
                sums = tuple(s + s for s in sums)
            sums = lax.fori_loop(jt * 8, jt * 8 + 8, inner, sums, unroll=4)
            for r in range(12):
                mine = got[pl.ds(jt * 8 * ROWS + h * 12 + r, 8, stride=ROWS), :]
                result = result + sums[r] * mine
    return result


def early_kernel(b_rows, w, moments):
    b = b_rows[0:24, :]
    moments[0:8, :] = fold(b * b)
    moments[8:16, :] = fold(b * w[...])
    moments[16:24, :] = fold(w[...] * w[...])


def third_kernel(freq, v, low, up, conn, hot, blocks, mass_row, w, early, got, line_out, stack):
    gather_blocks(v, low, up, conn, hot, stack, [(got, 0, ROWS)])
    last = quadratic(blocks, got)
    weights = edge_weights(freq, ROWS, 256)
    for t in range(8):
        cols = slice(t * 256, (t + 1) * 256)
        last = last + fold(weights * mass_row[0:1, cols] * v[:, cols] * v[:, cols])
    parts = [early[0:8, :], early[8:16, :], early[16:24, :], fold(w[...] * v[...]), fold(v[...] * v[...]), last]
    lane = lax.broadcasted_iota(i32, (1, LANES), 1)
    line = jnp.zeros((1, LANES), f32)
    for k, tile in enumerate(parts):
        line = line + jnp.where((lane & 7) == k, jnp.sum(tile), 0.0)
    line_out[...] = jnp.broadcast_to(line, (8, LANES))


def field_kernel(blocks, got, y):
    product(blocks, got, y, 2, 8, 4)


def gradients(got_rows, y, node_block, node_shape, energy, out, base):
    for jt in range(8):
        ys = [y[r * EB + jt * 8 : r * EB + jt * 8 + 8, :] for r in range(4)]
        for o in range(6):
            term = jnp.zeros((8, LANES), f32)
            for h in range(2):
                for c in range(2):
                    x = got_rows[pl.ds(jt * 8 * ROWS + h * 12 + o * 2 + c, 8, stride=ROWS), :]
                    term = term - x * ys[h * 2 + c] if c else term + x * ys[h * 2 + c]
            energy[o, jt * 8 : jt * 8 + 8, :] = term

    def body(c, carry):
        index = jnp.broadcast_to(node_block[pl.ds(c, 1), :], (8, LANES))
        cols = pl.ds(pl.multiple_of(c * LANES, LANES), LANES)
        sums = [jnp.zeros((8, LANES), f32) for _ in range(18)]
        for jt in range(8):
            shape = [node_shape[k, jt * 8 : jt * 8 + 8, cols] for k in range(3)]
            for o in range(6):
                x = jnp.take_along_axis(energy[o, jt * 8 : jt * 8 + 8, :], index, axis=1, mode="promise_in_bounds")
                for k in range(3):
                    sums[o * 3 + k] = sums[o * 3 + k] - shape[k] * x
        for q in range(18):
            out[c, base + q : base + q + 1, :] = jnp.sum(sums[q], axis=0, keepdims=True)
        return carry

    lax.fori_loop(0, 8, body, 0)


def early_gradient_kernel(got0, got1, y, node_block, node_shape, out, energy):
    gradients(got0, y, node_block, node_shape, energy, out, 0)
    gradients(got1, y, node_block, node_shape, energy, out, 18)
    out[:, 36:40, :] = jnp.zeros((8, 4, LANES), f32)


def late_gradient_kernel(early, got2, y, node_block, node_shape, line, out, energy):
    out[:, 0:40, :] = early[...]
    gradients(got2, y, node_block, node_shape, energy, out, 40)
    for c in range(8):
        out[c, 58:64, :] = line[0:6, :]


def message_kernel(shares, out):
    line = shares[0, 60:61, :]
    for d in range(1, 8):
        line = line + shares[d, 60:61, :]
    out[...] = jnp.broadcast_to(line, (32, LANES))


def last_kernel(messages, rows, w, v, shares, adjoint, gradient):
    line = jnp.sum(messages[...], axis=0, keepdims=True)
    lane = lax.broadcasted_iota(i32, (1, LANES), 1)

    def moment(k):
        return jnp.sum(jnp.where((lane & 7) == k, line, 0.0), axis=1, keepdims=True)

    m = [moment(k) for k in range(6)]
    a0 = m[0] / m[1]
    r1 = (None, -a0)
    rr1 = m[0] - 2.0 * a0 * m[1] + a0 * a0 * m[2]
    b0 = rr1 / m[0]
    d1 = (1.0 + b0, -a0)
    dad1 = d1[0] * d1[0] * m[1] + 2.0 * d1[0] * d1[1] * m[2] + d1[1] * d1[1] * m[3]
    a1 = rr1 / dad1
    r2 = (None, r1[1] - a1 * d1[0], -a1 * d1[1])
    rr2 = (
        m[0] + 2.0 * r2[1] * m[1] + (2.0 * r2[2] + r2[1] * r2[1]) * m[2]
        + 2.0 * r2[1] * r2[2] * m[3] + r2[2] * r2[2] * m[4]
    )
    b1 = rr2 / rr1
    d2 = (1.0 + b1 * d1[0], r2[1] + b1 * d1[1], r2[2])
    dad2 = (
        d2[0] * d2[0] * m[1] + 2.0 * d2[0] * d2[1] * m[2] + (2.0 * d2[0] * d2[2] + d2[1] * d2[1]) * m[3]
        + 2.0 * d2[1] * d2[2] * m[4] + d2[2] * d2[2] * m[5]
    )
    a2 = rr2 / dad2
    c0 = a0 + a1 * d1[0] + a2 * d2[0]
    c1 = a1 * d1[1] + a2 * d2[1]
    c2 = a2 * d2[2]
    for h in range(2):
        for o in range(6):
            at = slice(h * 12 + o * 2, h * 12 + o * 2 + 2)
            adjoint[h, o] = c0 * rows[at, :] + c1 * w[at, :] + c2 * v[at, :]
    share = shares[0]
    for d in range(1, 8):
        share = share + shares[d]
    for o in range(6):
        gradient[o] = (
            c0 * share[o * 3 : o * 3 + 3] + c1 * share[18 + o * 3 : 21 + o * 3] + c2 * share[40 + o * 3 : 43 + o * 3]
        )


def shifted(x, by):
    count = lax.axis_size("mesh")
    return lax.ppermute(x, "mesh", [(i, i + by) for i in range(count) if 0 <= i + by < count])


def exchanged(to_low, to_up):
    return shifted(to_up, 1), shifted(to_low, -1)


def per_device(
    adjoint_rhs, forward_field, stiffness, mass_blocks, frequency, edge_mass, connectivity, send_list, node_block, node_shape
):
    lists = send_list[0]
    mass_row = edge_mass.reshape(1, EDGES)
    nodes = node_block.reshape(8, LANES)
    ghosts = (arr(ROWS, SLOTS), arr(ROWS, SLOTS))
    got_shape = arr(EB * ROWS, LANES)
    medium = dict(flops=10**9, nbytes=10**7)

    rows, to_low, to_up = kernel_call(
        prep_kernel, "prep", (arr(32, EDGES), arr(32, SLOTS), arr(32, SLOTS)), [HBM] * 3,
        [
            pltpu.VMEM(adjoint_rhs.shape, f32),
            pltpu.VMEM(forward_field.shape, f32),
            pltpu.VMEM(lists.shape, i32),
            pltpu.SemaphoreType.DMA((3,)),
        ],
        flops=10**6, nbytes=10**6, limit=62,
    )(adjoint_rhs, forward_field, lists)
    low, up = exchanged(to_low, to_up)
    (hot,) = kernel_call(
        hot_kernel, "hot", (jax.ShapeDtypeStruct((WIDE, EB * LANES), bf16),), [VMEM], **medium
    )(connectivity)
    (blocks,) = kernel_call(blocks_kernel, "blocks", (arr(2, EB, EB, LANES),), [SMEM] + [VMEM] * 2, **medium)(
        frequency, stiffness, mass_blocks
    )

    def applied(x, low, up, with_field):
        count = 2 * PARTS * x.shape[0]
        terms, to_low, to_up, *got = kernel_call(
            functools.partial(apply_kernel, with_field), "apply",
            (arr(ROWS * EB, LANES),) + ghosts + (got_shape,) + (arr(EB * 8, LANES),) * with_field, [VMEM] * 6,
            [
                pltpu.VMEM((count, WIDE), bf16),
                pltpu.VMEM((2 * 48, CHUNK * LANES), bf16),
                pltpu.VMEM((2 * 48, WIDE), f32),
            ],
            **medium,
        )(x, low, up, connectivity, hot, blocks)
        from_low, from_up = exchanged(to_low, to_up)
        (p,) = kernel_call(
            sums_kernel, "sums", (arr(ROWS, EDGES),), [SMEM] + [VMEM] * 5,
            [pltpu.VMEM((4 * 48, CHUNK * LANES), bf16), pltpu.VMEM((4 * 48, WIDE), f32)], **medium,
        )(frequency, terms, connectivity, hot, x, mass_row)
        own, to_low, to_up = kernel_call(
            finish_kernel, "finish", (arr(ROWS, EDGES),) + ghosts, [VMEM] * 4, flops=10**7, nbytes=10**6
        )(p, lists, from_low, from_up)
        return got, own, exchanged(to_low, to_up)

    (got0, got_field), w, (low, up) = applied(rows, low, up, True)
    (y,) = kernel_call(field_kernel, "field", (arr(4 * EB, LANES),), [VMEM] * 2, **medium)(blocks, got_field)
    (got1,), v, (low, up) = applied(w, low, up, False)
    (grads,) = kernel_call(
        early_gradient_kernel, "early_gradient", (arr(8, 40, LANES),), [VMEM] * 5, [pltpu.VMEM((6, EB, LANES), f32)], **medium
    )(got0, got1, y, nodes, node_shape)
    (early,) = kernel_call(early_kernel, "early", (arr(24, LANES),), [VMEM] * 2, flops=10**6, nbytes=10**6)(rows, w)
    got2, line = kernel_call(
        third_kernel, "third", (got_shape, arr(8, LANES)), [SMEM] + [VMEM] * 9,
        [pltpu.VMEM((PARTS * 48, WIDE), bf16)], **medium,
    )(frequency, v, low, up, connectivity, hot, blocks, mass_row, w, early)
    (grads,) = kernel_call(
        late_gradient_kernel, "late_gradient", (arr(8, 64, LANES),), [VMEM] * 6, [pltpu.VMEM((6, EB, LANES), f32)], **medium
    )(grads, got2, y, nodes, node_shape, line)
    shares = lax.all_to_all(grads, "harm", 0, 0, tiled=True)
    (message,) = kernel_call(message_kernel, "message", (arr(32, LANES),), [VMEM], flops=10**3, nbytes=10**5)(shares)
    messages = lax.all_to_all(message.reshape(32 * LANES), "mesh", 0, 0, tiled=True).reshape(32, LANES)
    adjoint, gradient = kernel_call(
        last_kernel, "last", (arr(*adjoint_rhs.shape), arr(6, 3, LANES)), [VMEM] * 5, flops=10**6, nbytes=10**6
    )(messages, rows, w, v, shares)
    return adjoint, gradient


def solution(mesh):
    return jax.shard_map(
        per_device,
        mesh=mesh,
        in_specs=(
            P("harm", None, None, "mesh"),
            P("harm", None, "mesh"),
            P(None, None, "mesh"),
            P(None, None, "mesh"),
            P("harm"),
            P("mesh"),
            P(None, "mesh"),
            P("mesh", None, None),
            P("mesh"),
            P(None, None, "mesh"),
        ),
        out_specs=(P("harm", None, None, "mesh"), P(None, None, ("mesh", "harm"))),
        check_vma=False,
    )
```

```python
import functools

import jax
import jax.numpy as jnp
from jax import lax
from jax.experimental import pallas as pl
from jax.experimental.pallas import tpu as pltpu
from jax.sharding import PartitionSpec as P

f32 = jnp.float32
bf16 = jnp.bfloat16
i32 = jnp.int32
LANES = 128
EDGES = 2048
SLOTS = 512
ROWS = 24
EB = 64
OWN_T, GHOST_T = EDGES // LANES, SLOTS // LANES
BOTH = ("mesh", "harm")

VMEM = pl.BlockSpec(memory_space=pltpu.VMEM)
SMEM = pl.BlockSpec(memory_space=pltpu.SMEM)
HBM = pl.BlockSpec(memory_space=pltpu.HBM)


def kernel_call(body, name, out, specs, scratch=(), flops=0, nbytes=0, limit=20):
    return pl.pallas_call(
        body,
        name=name,
        out_shape=out,
        in_specs=specs,
        out_specs=jax.tree.map(lambda _: VMEM, out),
        scratch_shapes=scratch,
        compiler_params=pltpu.CompilerParams(vmem_limit_bytes=limit * 2**20),
        cost_estimate=pl.CostEstimate(flops=flops, bytes_accessed=nbytes, transcendentals=0),
    )


def arr(*shape):
    return jax.ShapeDtypeStruct(shape, f32)


def lookup(tables, index):
    lane = jnp.broadcast_to(index & (LANES - 1), (8, LANES))
    high = jnp.broadcast_to(index >> 7, (8, LANES))
    found = [jnp.take_along_axis(t, lane, axis=1, mode="promise_in_bounds") for t in tables]
    bit = 1
    while len(found) > 1:
        odd = (high & bit) != 0
        found = [
            jnp.where(odd, found[a + 1], found[a]) if a + 1 < len(found) else found[a]
            for a in range(0, len(found), 2)
        ]
        bit *= 2
    return found[0]


def tiles(ref, row, count):
    return [ref[row : row + 8, t * LANES : (t + 1) * LANES] for t in range(count)]


WIDE = 512
PARTS = (EDGES + 2 * SLOTS) // WIDE
CHUNK = 16


def gather_blocks(own, low, up, conn, hot, stack, outs):
    count = own.shape[0]
    for t in range(PARTS):
        x = own[:, t * WIDE : (t + 1) * WIDE] if t < PARTS - 2 else (low if t == PARTS - 2 else up)[...]
        stack[t * 2 * count : (t + 1) * 2 * count, :] = pieces(x)

    def body(c, carry):
        cols = pl.ds(pl.multiple_of(c * CHUNK * LANES, CHUNK * LANES), CHUNK * LANES)
        found = jnp.dot(stack[...], hot[:, cols], preferred_element_type=f32)
        for jj in range(CHUNK):
            j = c * CHUNK + jj
            high = conn[pl.ds(j, 1), :] >> 9
            for out, first, rows in outs:
                value = None
                for t in range(PARTS):
                    at = t * 2 * count + first
                    lanes = slice(jj * LANES, (jj + 1) * LANES)
                    x = found[at : at + rows, lanes] + found[at + count : at + count + rows, lanes]
                    value = x if t == 0 else jnp.where(jnp.broadcast_to(high, x.shape) == t, x, value)
                out[pl.ds(pl.multiple_of(j * rows, 8), rows), :] = value
        return carry

    lax.fori_loop(0, EB // CHUNK, body, 0)


def product(blocks, got, out, per_harm, per_edge, wide):
    for h in range(2):

        def outer(jt, carry):
            def inner(i, sums):
                ks = []
                for q in range(wide):
                    rows = pl.ds(pl.multiple_of((jt * wide + q) * 8, 8), 8)
                    ks.append(blocks[h, i, rows, :])
                new = []
                for r in range(per_harm):
                    x = jnp.broadcast_to(got[pl.ds(i * per_edge + h * per_harm + r, 1), :], (8, LANES))
                    for q in range(wide):
                        new.append(sums[r * wide + q] + ks[q] * x)
                return tuple(new)

            zero = jnp.zeros((8, LANES), f32)
            sums = lax.fori_loop(0, EB, inner, (zero,) * (per_harm * wide), unroll=8)
            for r in range(per_harm):
                for q in range(wide):
                    at = (h * per_harm + r) * EB + (jt * wide + q) * 8
                    out[pl.ds(pl.multiple_of(at, 8), 8), :] = sums[r * wide + q]
            return carry

        lax.fori_loop(0, EB // (8 * wide), outer, 0)


def pieces(x):
    high = x.astype(bf16).astype(f32)
    return jnp.concatenate([high, x - high], axis=0).astype(bf16)


def one_hot_low(index):
    low = jnp.broadcast_to(index & 255, (256, LANES))
    return jnp.where(low == lax.broadcasted_iota(i32, (256, LANES), 0), 1.0, 0.0).astype(bf16)


def masked_stack(parts, index, first, last):
    high = index >> 8
    stack = []
    for t in range(first, last):
        mask = jnp.broadcast_to(jnp.where(high == t, 1.0, 0.0), parts.shape).astype(bf16)
        stack.append(parts * mask)
    return stack


def add_up(stack, hot):
    return lax.dot_general(stack, hot, (((1,), (1,)), ((), ())), preferred_element_type=f32)


def scatter_blocks(terms, conn, hot, stack, total):
    total[...] = jnp.zeros_like(total)
    for c in range(EB // CHUNK):

        def body(jj, carry):
            j = c * CHUNK + jj
            cols = pl.ds(pl.multiple_of(jj * LANES, LANES), LANES)
            x = terms[pl.ds(j, ROWS, stride=EB), :]
            first = x.astype(bf16).astype(f32)
            rest = x - first
            high = jnp.broadcast_to(conn[pl.ds(j, 1), :] >> 9, (ROWS, LANES))
            for t in range(PARTS):
                here = high == t
                both = jnp.concatenate([jnp.where(here, first, 0.0), jnp.where(here, rest, 0.0)], axis=0)
                stack[t * 48 : t * 48 + 48, cols] = both.astype(bf16)
            return carry

        lax.fori_loop(0, CHUNK, body, 0, unroll=CHUNK)
        total[...] += add_up(stack[...], hot[:, c * CHUNK * LANES : (c + 1) * CHUNK * LANES])


def total_tile(total, t):
    return total[t * 48 : t * 48 + 24, :] + total[t * 48 + 24 : t * 48 + 48, :]


def edge_weights(freq, rows, width):
    upper = lax.broadcasted_iota(i32, (rows, width), 0) < rows // 2
    return jnp.where(upper, freq[0], freq[1])


def pick_listed(source, lists, outs, groups):
    for side in range(2):
        for c in range(GHOST_T):
            cols = slice(c * LANES, (c + 1) * LANES)
            index = lists[side : side + 1, cols]
            for g in range(groups):
                value = lookup(tiles(source, g * 8, OWN_T), index)
                outs[side][g * 8 : g * 8 + 8, cols] = jnp.where(index >= 0, value, 0.0)


def fold(x):
    rows, cols = x.shape
    total = jnp.zeros((8, LANES), f32)
    for r in range(rows // 8):
        for c in range(cols // LANES):
            total = total + x[r * 8 : r * 8 + 8, c * LANES : (c + 1) * LANES]
    return total


def prep_kernel(rhs_in, field_in, lists_in, rows, to_low, to_up, rhs, field, lists, sems):
    copies = [
        pltpu.make_async_copy(a, b, sems.at[k])
        for k, (a, b) in enumerate(((rhs_in, rhs), (field_in, field), (lists_in, lists)))
    ]
    for copy in copies:
        copy.start()
    for copy in copies:
        copy.wait()
    for h in range(2):
        for o in range(6):
            at = h * 12 + o * 2
            rows[at : at + 2, :] = rhs[h, o]
        rows[24 + 2 * h : 26 + 2 * h, :] = field[h]
    rows[28:32, :] = jnp.zeros((4, EDGES), f32)
    pick_listed(rows, lists, (to_low, to_up), 4)


def hot_kernel(conn, hot):
    half = WIDE // 2

    def body(j, carry):
        index = conn[pl.ds(j, 1), :]
        cols = pl.ds(pl.multiple_of(j * LANES, LANES), LANES)
        low = jnp.broadcast_to(index & (half - 1), (half, LANES))
        one = jnp.where(low == lax.broadcasted_iota(i32, (half, LANES), 0), 1.0, 0.0).astype(bf16)
        upper = jnp.broadcast_to(jnp.where((index & half) != 0, 1.0, 0.0), (16, LANES))
        upper, lower = upper.astype(bf16), (1.0 - upper).astype(bf16)
        for q in range(half // 16):
            part = one[q * 16 : q * 16 + 16]
            hot[q * 16 : q * 16 + 16, cols] = part * lower
            hot[half + q * 16 : half + q * 16 + 16, cols] = part * upper
        return carry

    lax.fori_loop(0, EB, body, 0, unroll=8)


def blocks_kernel(freq, stiff, mass, blocks):
    def body(i, carry):
        for h in range(2):
            blocks[h, i] = stiff[i] + freq[h] * mass[i]
        return carry

    lax.fori_loop(0, EB, body, 0, unroll=2)


def apply_kernel(with_field, freq, own, low, up, conn, hot, blocks, mass_row, p, to_low, to_up, got, *refs):
    stack, terms, masked, total = refs[-4:]
    outs = [(got, 0, ROWS)] + ([(refs[0], ROWS, 8)] if with_field else [])
    gather_blocks(own, low, up, conn, hot, stack, outs)
    product(blocks, got, terms, 12, ROWS, 2)
    scatter_blocks(terms, conn, hot, masked, total)
    weights = edge_weights(freq, ROWS, WIDE)
    for t in range(PARTS):
        sums = total[t * 48 : t * 48 + 24, :] + total[t * 48 + 24 : t * 48 + 48, :]
        if t < PARTS - 2:
            cols = slice(t * WIDE, (t + 1) * WIDE)
            p[:, cols] = sums + weights * mass_row[0:1, cols] * own[0:ROWS, cols]
        else:
            (to_low if t == PARTS - 2 else to_up)[...] = sums


def finish_kernel(p, lists, from_low, from_up, own, to_low, to_up):
    arrived = jnp.concatenate([from_low[...], from_up[...]], axis=1)
    hots, stacks = [], []
    for c in range(2 * GHOST_T):
        index = lists[c // GHOST_T : c // GHOST_T + 1, (c % GHOST_T) * LANES : (c % GHOST_T + 1) * LANES]
        hots.append(one_hot_low(index))
        parts = pieces(arrived[:, c * LANES : (c + 1) * LANES])
        stacks.append(jnp.concatenate(masked_stack(parts, index, 0, 8), axis=0))
    sums = add_up(jnp.concatenate(stacks, axis=1), jnp.concatenate(hots, axis=1))
    for t in range(8):
        own[:, t * 256 : (t + 1) * 256] = p[:, t * 256 : (t + 1) * 256] + total_tile(sums, t)
    pick_listed(own, lists, (to_low, to_up), 3)


def quadratic(blocks, got):
    result = jnp.zeros((8, LANES), f32)
    for h in range(2):
        for jt in range(8):

            def inner(i, sums):
                k = blocks[h, i, jt * 8 : jt * 8 + 8, :]
                return tuple(
                    s + k * jnp.broadcast_to(got[pl.ds(i * ROWS + h * 12 + r, 1), :], (8, LANES))
                    for r, s in enumerate(sums)
                )

            zero = jnp.zeros((8, LANES), f32)
            sums = (zero,) * 12
            if jt < 7:
                sums = lax.fori_loop(jt * 8 + 8, EB, inner, sums, unroll=4)
                sums = tuple(s + s for s in sums)
            sums = lax.fori_loop(jt * 8, jt * 8 + 8, inner, sums, unroll=4)
            for r in range(12):
                mine = got[pl.ds(jt * 8 * ROWS + h * 12 + r, 8, stride=ROWS), :]
                result = result + sums[r] * mine
    return result


def early_kernel(b_rows, w, moments):
    b = b_rows[0:24, :]
    moments[0:8, :] = fold(b * b)
    moments[8:16, :] = fold(b * w[...])
    moments[16:24, :] = fold(w[...] * w[...])


def third_kernel(freq, v, low, up, conn, hot, blocks, mass_row, w, early, got, line_out, stack):
    gather_blocks(v, low, up, conn, hot, stack, [(got, 0, ROWS)])
    last = quadratic(blocks, got)
    weights = edge_weights(freq, ROWS, 256)
    for t in range(8):
        cols = slice(t * 256, (t + 1) * 256)
        last = last + fold(weights * mass_row[0:1, cols] * v[:, cols] * v[:, cols])
    parts = [early[0:8, :], early[8:16, :], early[16:24, :], fold(w[...] * v[...]), fold(v[...] * v[...]), last]
    lane = lax.broadcasted_iota(i32, (1, LANES), 1)
    line = jnp.zeros((1, LANES), f32)
    for k, tile in enumerate(parts):
        line = line + jnp.where((lane & 7) == k, jnp.sum(tile), 0.0)
    line_out[...] = jnp.broadcast_to(line, (8, LANES))


def field_kernel(blocks, got, y):
    product(blocks, got, y, 2, 8, 4)


def gradients(got_rows, y, node_block, node_shape, energy, out, base):
    for jt in range(8):
        ys = [y[r * EB + jt * 8 : r * EB + jt * 8 + 8, :] for r in range(4)]
        for o in range(6):
            term = jnp.zeros((8, LANES), f32)
            for h in range(2):
                for c in range(2):
                    x = got_rows[pl.ds(jt * 8 * ROWS + h * 12 + o * 2 + c, 8, stride=ROWS), :]
                    term = term - x * ys[h * 2 + c] if c else term + x * ys[h * 2 + c]
            energy[o, jt * 8 : jt * 8 + 8, :] = term

    def body(c, carry):
        index = jnp.broadcast_to(node_block[pl.ds(c, 1), :], (8, LANES))
        cols = pl.ds(pl.multiple_of(c * LANES, LANES), LANES)
        sums = [jnp.zeros((8, LANES), f32) for _ in range(18)]
        for jt in range(8):
            shape = [node_shape[k, jt * 8 : jt * 8 + 8, cols] for k in range(3)]
            for o in range(6):
                x = jnp.take_along_axis(energy[o, jt * 8 : jt * 8 + 8, :], index, axis=1, mode="promise_in_bounds")
                for k in range(3):
                    sums[o * 3 + k] = sums[o * 3 + k] - shape[k] * x
        for q in range(18):
            out[c, base + q : base + q + 1, :] = jnp.sum(sums[q], axis=0, keepdims=True)
        return carry

    lax.fori_loop(0, 8, body, 0)


def early_gradient_kernel(got0, got1, y, node_block, node_shape, out, energy):
    gradients(got0, y, node_block, node_shape, energy, out, 0)
    gradients(got1, y, node_block, node_shape, energy, out, 18)
    out[:, 36:40, :] = jnp.zeros((8, 4, LANES), f32)


def late_gradient_kernel(early, got2, y, node_block, node_shape, line, out, energy):
    out[:, 0:40, :] = early[...]
    gradients(got2, y, node_block, node_shape, energy, out, 40)
    for c in range(8):
        out[c, 58:64, :] = line[0:6, :]


def message_kernel(shares, out):
    line = shares[0, 60:61, :]
    for d in range(1, 8):
        line = line + shares[d, 60:61, :]
    out[...] = jnp.broadcast_to(line, (32, LANES))


def last_kernel(messages, rows, w, v, shares, adjoint, gradient):
    line = jnp.sum(messages[...], axis=0, keepdims=True)
    lane = lax.broadcasted_iota(i32, (1, LANES), 1)

    def moment(k):
        return jnp.sum(jnp.where((lane & 7) == k, line, 0.0), axis=1, keepdims=True)

    m = [moment(k) for k in range(6)]
    a0 = m[0] / m[1]
    r1 = (None, -a0)
    rr1 = m[0] - 2.0 * a0 * m[1] + a0 * a0 * m[2]
    b0 = rr1 / m[0]
    d1 = (1.0 + b0, -a0)
    dad1 = d1[0] * d1[0] * m[1] + 2.0 * d1[0] * d1[1] * m[2] + d1[1] * d1[1] * m[3]
    a1 = rr1 / dad1
    r2 = (None, r1[1] - a1 * d1[0], -a1 * d1[1])
    rr2 = (
        m[0] + 2.0 * r2[1] * m[1] + (2.0 * r2[2] + r2[1] * r2[1]) * m[2]
        + 2.0 * r2[1] * r2[2] * m[3] + r2[2] * r2[2] * m[4]
    )
    b1 = rr2 / rr1
    d2 = (1.0 + b1 * d1[0], r2[1] + b1 * d1[1], r2[2])
    dad2 = (
        d2[0] * d2[0] * m[1] + 2.0 * d2[0] * d2[1] * m[2] + (2.0 * d2[0] * d2[2] + d2[1] * d2[1]) * m[3]
        + 2.0 * d2[1] * d2[2] * m[4] + d2[2] * d2[2] * m[5]
    )
    a2 = rr2 / dad2
    c0 = a0 + a1 * d1[0] + a2 * d2[0]
    c1 = a1 * d1[1] + a2 * d2[1]
    c2 = a2 * d2[2]
    for h in range(2):
        for o in range(6):
            at = slice(h * 12 + o * 2, h * 12 + o * 2 + 2)
            adjoint[h, o] = c0 * rows[at, :] + c1 * w[at, :] + c2 * v[at, :]
    share = shares[0]
    for d in range(1, 8):
        share = share + shares[d]
    for o in range(6):
        gradient[o] = (
            c0 * share[o * 3 : o * 3 + 3] + c1 * share[18 + o * 3 : 21 + o * 3] + c2 * share[40 + o * 3 : 43 + o * 3]
        )


def shifted(x, by):
    count = lax.axis_size("mesh")
    return lax.ppermute(x, "mesh", [(i, i + by) for i in range(count) if 0 <= i + by < count])


def exchanged(to_low, to_up):
    return shifted(to_up, 1), shifted(to_low, -1)


def per_device(
    adjoint_rhs, forward_field, stiffness, mass_blocks, frequency, edge_mass, connectivity, send_list, node_block, node_shape
):
    lists = send_list[0]
    mass_row = edge_mass.reshape(1, EDGES)
    nodes = node_block.reshape(8, LANES)
    ghosts = (arr(ROWS, SLOTS), arr(ROWS, SLOTS))
    got_shape = arr(EB * ROWS, LANES)
    medium = dict(flops=10**9, nbytes=10**7)

    rows, to_low, to_up = kernel_call(
        prep_kernel, "prep", (arr(32, EDGES), arr(32, SLOTS), arr(32, SLOTS)), [HBM] * 3,
        [
            pltpu.VMEM(adjoint_rhs.shape, f32),
            pltpu.VMEM(forward_field.shape, f32),
            pltpu.VMEM(lists.shape, i32),
            pltpu.SemaphoreType.DMA((3,)),
        ],
        flops=10**6, nbytes=10**6, limit=62,
    )(adjoint_rhs, forward_field, lists)
    low, up = exchanged(to_low, to_up)
    (hot,) = kernel_call(
        hot_kernel, "hot", (jax.ShapeDtypeStruct((WIDE, EB * LANES), bf16),), [VMEM], **medium
    )(connectivity)
    (blocks,) = kernel_call(blocks_kernel, "blocks", (arr(2, EB, EB, LANES),), [SMEM] + [VMEM] * 2, **medium)(
        frequency, stiffness, mass_blocks
    )

    def applied(x, low, up, with_field):
        count = 2 * PARTS * x.shape[0]
        p, to_low, to_up, *got = kernel_call(
            functools.partial(apply_kernel, with_field), "apply",
            (arr(ROWS, EDGES),) + ghosts + (got_shape,) + (arr(EB * 8, LANES),) * with_field, [SMEM] + [VMEM] * 7,
            [
                pltpu.VMEM((count, WIDE), bf16),
                pltpu.VMEM((ROWS * EB, LANES), f32),
                pltpu.VMEM((PARTS * 48, CHUNK * LANES), bf16),
                pltpu.VMEM((PARTS * 48, WIDE), f32),
            ],
            **medium,
        )(frequency, x, low, up, connectivity, hot, blocks, mass_row)
        from_low, from_up = exchanged(to_low, to_up)
        own, to_low, to_up = kernel_call(
            finish_kernel, "finish", (arr(ROWS, EDGES),) + ghosts, [VMEM] * 4, flops=10**7, nbytes=10**6
        )(p, lists, from_low, from_up)
        return got, own, exchanged(to_low, to_up)

    (got0, got_field), w, (low, up) = applied(rows, low, up, True)
    (y,) = kernel_call(field_kernel, "field", (arr(4 * EB, LANES),), [VMEM] * 2, **medium)(blocks, got_field)
    (got1,), v, (low, up) = applied(w, low, up, False)
    (grads,) = kernel_call(
        early_gradient_kernel, "early_gradient", (arr(8, 40, LANES),), [VMEM] * 5, [pltpu.VMEM((6, EB, LANES), f32)], **medium
    )(got0, got1, y, nodes, node_shape)
    (early,) = kernel_call(early_kernel, "early", (arr(24, LANES),), [VMEM] * 2, flops=10**6, nbytes=10**6)(rows, w)
    got2, line = kernel_call(
        third_kernel, "third", (got_shape, arr(8, LANES)), [SMEM] + [VMEM] * 9,
        [pltpu.VMEM((PARTS * 48, WIDE), bf16)], **medium,
    )(frequency, v, low, up, connectivity, hot, blocks, mass_row, w, early)
    (grads,) = kernel_call(
        late_gradient_kernel, "late_gradient", (arr(8, 64, LANES),), [VMEM] * 6, [pltpu.VMEM((6, EB, LANES), f32)], **medium
    )(grads, got2, y, nodes, node_shape, line)
    shares = lax.all_to_all(grads, "harm", 0, 0, tiled=True)
    (message,) = kernel_call(message_kernel, "message", (arr(32, LANES),), [VMEM], flops=10**3, nbytes=10**5)(shares)
    messages = lax.all_to_all(message.reshape(32 * LANES), "mesh", 0, 0, tiled=True).reshape(32, LANES)
    adjoint, gradient = kernel_call(
        last_kernel, "last", (arr(*adjoint_rhs.shape), arr(6, 3, LANES)), [VMEM] * 5, flops=10**6, nbytes=10**6
    )(messages, rows, w, v, shares)
    return adjoint, gradient


def solution(mesh):
    return jax.shard_map(
        per_device,
        mesh=mesh,
        in_specs=(
            P("harm", None, None, "mesh"),
            P("harm", None, "mesh"),
            P(None, None, "mesh"),
            P(None, None, "mesh"),
            P("harm"),
            P("mesh"),
            P(None, "mesh"),
            P("mesh", None, None),
            P("mesh"),
            P(None, None, "mesh"),
        ),
        out_specs=(P("harm", None, None, "mesh"), P(None, None, ("mesh", "harm"))),
        check_vma=False,
    )
```

```python
import functools

import jax
import jax.numpy as jnp
from jax import lax
from jax.experimental import pallas as pl
from jax.experimental.pallas import tpu as pltpu
from jax.sharding import PartitionSpec as P

f32 = jnp.float32
bf16 = jnp.bfloat16
i32 = jnp.int32
LANES = 128
EDGES = 2048
SLOTS = 512
ROWS = 24
EB = 64
OWN_T, GHOST_T = EDGES // LANES, SLOTS // LANES
BOTH = ("mesh", "harm")

VMEM = pl.BlockSpec(memory_space=pltpu.VMEM)
SMEM = pl.BlockSpec(memory_space=pltpu.SMEM)
HBM = pl.BlockSpec(memory_space=pltpu.HBM)


def kernel_call(body, name, out, specs, scratch=(), flops=0, nbytes=0, limit=20):
    return pl.pallas_call(
        body,
        name=name,
        out_shape=out,
        in_specs=specs,
        out_specs=jax.tree.map(lambda _: VMEM, out),
        scratch_shapes=scratch,
        compiler_params=pltpu.CompilerParams(vmem_limit_bytes=limit * 2**20),
        cost_estimate=pl.CostEstimate(flops=flops, bytes_accessed=nbytes, transcendentals=0),
    )


def arr(*shape):
    return jax.ShapeDtypeStruct(shape, f32)


def lookup(tables, index):
    lane = jnp.broadcast_to(index & (LANES - 1), (8, LANES))
    high = jnp.broadcast_to(index >> 7, (8, LANES))
    found = [jnp.take_along_axis(t, lane, axis=1, mode="promise_in_bounds") for t in tables]
    bit = 1
    while len(found) > 1:
        odd = (high & bit) != 0
        found = [
            jnp.where(odd, found[a + 1], found[a]) if a + 1 < len(found) else found[a]
            for a in range(0, len(found), 2)
        ]
        bit *= 2
    return found[0]


def tiles(ref, row, count):
    return [ref[row : row + 8, t * LANES : (t + 1) * LANES] for t in range(count)]


WIDE = 512
PARTS = (EDGES + 2 * SLOTS) // WIDE
CHUNK = 16


def gather_blocks(own, low, up, conn, hot, stack, outs):
    count = own.shape[0]
    for t in range(PARTS):
        x = own[:, t * WIDE : (t + 1) * WIDE] if t < PARTS - 2 else (low if t == PARTS - 2 else up)[...]
        stack[t * 2 * count : (t + 1) * 2 * count, :] = pieces(x)

    for c in range(EB // CHUNK):
        found = jnp.dot(stack[...], hot[:, c * CHUNK * LANES : (c + 1) * CHUNK * LANES], preferred_element_type=f32)
        for jj in range(CHUNK):
            j = c * CHUNK + jj
            high = conn[j : j + 1, :] >> 9
            for out, first, rows in outs:
                value = None
                for t in range(PARTS):
                    at = t * 2 * count + first
                    lanes = slice(jj * LANES, (jj + 1) * LANES)
                    x = found[at : at + rows, lanes] + found[at + count : at + count + rows, lanes]
                    value = x if t == 0 else jnp.where(jnp.broadcast_to(high, x.shape) == t, x, value)
                out[j * rows : (j + 1) * rows, :] = value


def product(blocks, got, out, per_harm, per_edge, wide):
    for h in range(2):

        def outer(jt, carry):
            def inner(i, sums):
                ks = []
                for q in range(wide):
                    rows = pl.ds(pl.multiple_of((jt * wide + q) * 8, 8), 8)
                    ks.append(blocks[h, i, rows, :])
                new = []
                for r in range(per_harm):
                    x = jnp.broadcast_to(got[pl.ds(i * per_edge + h * per_harm + r, 1), :], (8, LANES))
                    for q in range(wide):
                        new.append(sums[r * wide + q] + ks[q] * x)
                return tuple(new)

            zero = jnp.zeros((8, LANES), f32)
            sums = lax.fori_loop(0, EB, inner, (zero,) * (per_harm * wide), unroll=8)
            for r in range(per_harm):
                for q in range(wide):
                    at = (h * per_harm + r) * EB + (jt * wide + q) * 8
                    out[pl.ds(pl.multiple_of(at, 8), 8), :] = sums[r * wide + q]
            return carry

        lax.fori_loop(0, EB // (8 * wide), outer, 0)


def pieces(x):
    high = x.astype(bf16).astype(f32)
    return jnp.concatenate([high, x - high], axis=0).astype(bf16)


def one_hot_low(index):
    low = jnp.broadcast_to(index & 255, (256, LANES))
    return jnp.where(low == lax.broadcasted_iota(i32, (256, LANES), 0), 1.0, 0.0).astype(bf16)


def masked_stack(parts, index, first, last):
    high = index >> 8
    stack = []
    for t in range(first, last):
        mask = jnp.broadcast_to(jnp.where(high == t, 1.0, 0.0), parts.shape).astype(bf16)
        stack.append(parts * mask)
    return stack


def add_up(stack, hot):
    return lax.dot_general(stack, hot, (((1,), (1,)), ((), ())), preferred_element_type=f32)


def scatter_blocks(terms, conn, hot, stack, total):
    total[...] = jnp.zeros_like(total)
    for c in range(EB // CHUNK):

        def body(jj, carry):
            j = c * CHUNK + jj
            cols = pl.ds(pl.multiple_of(jj * LANES, LANES), LANES)
            x = terms[pl.ds(j, ROWS, stride=EB), :]
            first = x.astype(bf16).astype(f32)
            rest = x - first
            high = jnp.broadcast_to(conn[pl.ds(j, 1), :] >> 9, (ROWS, LANES))
            for t in range(PARTS):
                here = high == t
                both = jnp.concatenate([jnp.where(here, first, 0.0), jnp.where(here, rest, 0.0)], axis=0)
                stack[t * 48 : t * 48 + 48, cols] = both.astype(bf16)
            return carry

        lax.fori_loop(0, CHUNK, body, 0, unroll=CHUNK)
        total[...] += add_up(stack[...], hot[:, c * CHUNK * LANES : (c + 1) * CHUNK * LANES])


def total_tile(total, t):
    return total[t * 48 : t * 48 + 24, :] + total[t * 48 + 24 : t * 48 + 48, :]


def edge_weights(freq, rows, width):
    upper = lax.broadcasted_iota(i32, (rows, width), 0) < rows // 2
    return jnp.where(upper, freq[0], freq[1])


def pick_listed(source, lists, outs, groups):
    for side in range(2):
        for c in range(GHOST_T):
            cols = slice(c * LANES, (c + 1) * LANES)
            index = lists[side : side + 1, cols]
            for g in range(groups):
                value = lookup(tiles(source, g * 8, OWN_T), index)
                outs[side][g * 8 : g * 8 + 8, cols] = jnp.where(index >= 0, value, 0.0)


def fold(x):
    rows, cols = x.shape
    total = jnp.zeros((8, LANES), f32)
    for r in range(rows // 8):
        for c in range(cols // LANES):
            total = total + x[r * 8 : r * 8 + 8, c * LANES : (c + 1) * LANES]
    return total


def prep_kernel(rhs_in, field_in, lists_in, rows, to_low, to_up, rhs, field, lists, sems):
    copies = [
        pltpu.make_async_copy(a, b, sems.at[k])
        for k, (a, b) in enumerate(((rhs_in, rhs), (field_in, field), (lists_in, lists)))
    ]
    for copy in copies:
        copy.start()
    for copy in copies:
        copy.wait()
    for h in range(2):
        for o in range(6):
            at = h * 12 + o * 2
            rows[at : at + 2, :] = rhs[h, o]
        rows[24 + 2 * h : 26 + 2 * h, :] = field[h]
    rows[28:32, :] = jnp.zeros((4, EDGES), f32)
    pick_listed(rows, lists, (to_low, to_up), 4)


def hot_kernel(conn, hot):
    half = WIDE // 2

    def body(j, carry):
        index = conn[pl.ds(j, 1), :]
        cols = pl.ds(pl.multiple_of(j * LANES, LANES), LANES)
        low = jnp.broadcast_to(index & (half - 1), (half, LANES))
        one = jnp.where(low == lax.broadcasted_iota(i32, (half, LANES), 0), 1.0, 0.0).astype(bf16)
        upper = jnp.broadcast_to(jnp.where((index & half) != 0, 1.0, 0.0), (16, LANES))
        upper, lower = upper.astype(bf16), (1.0 - upper).astype(bf16)
        for q in range(half // 16):
            part = one[q * 16 : q * 16 + 16]
            hot[q * 16 : q * 16 + 16, cols] = part * lower
            hot[half + q * 16 : half + q * 16 + 16, cols] = part * upper
        return carry

    lax.fori_loop(0, EB, body, 0, unroll=8)


def blocks_kernel(freq, stiff, mass, blocks):
    def body(i, carry):
        for h in range(2):
            blocks[h, i] = stiff[i] + freq[h] * mass[i]
        return carry

    lax.fori_loop(0, EB, body, 0, unroll=2)


def apply_kernel(with_field, freq, own, low, up, conn, hot, blocks, mass_row, p, to_low, to_up, got, *refs):
    stack, terms, masked, total = refs[-4:]
    outs = [(got, 0, ROWS)] + ([(refs[0], ROWS, 8)] if with_field else [])
    gather_blocks(own, low, up, conn, hot, stack, outs)
    product(blocks, got, terms, 12, ROWS, 2)
    scatter_blocks(terms, conn, hot, masked, total)
    weights = edge_weights(freq, ROWS, WIDE)
    for t in range(PARTS):
        sums = total[t * 48 : t * 48 + 24, :] + total[t * 48 + 24 : t * 48 + 48, :]
        if t < PARTS - 2:
            cols = slice(t * WIDE, (t + 1) * WIDE)
            p[:, cols] = sums + weights * mass_row[0:1, cols] * own[0:ROWS, cols]
        else:
            (to_low if t == PARTS - 2 else to_up)[...] = sums


def finish_kernel(p, lists, from_low, from_up, own, to_low, to_up):
    arrived = jnp.concatenate([from_low[...], from_up[...]], axis=1)
    hots, stacks = [], []
    for c in range(2 * GHOST_T):
        index = lists[c // GHOST_T : c // GHOST_T + 1, (c % GHOST_T) * LANES : (c % GHOST_T + 1) * LANES]
        hots.append(one_hot_low(index))
        parts = pieces(arrived[:, c * LANES : (c + 1) * LANES])
        stacks.append(jnp.concatenate(masked_stack(parts, index, 0, 8), axis=0))
    sums = add_up(jnp.concatenate(stacks, axis=1), jnp.concatenate(hots, axis=1))
    for t in range(8):
        own[:, t * 256 : (t + 1) * 256] = p[:, t * 256 : (t + 1) * 256] + total_tile(sums, t)
    pick_listed(own, lists, (to_low, to_up), 3)


def quadratic(blocks, got):
    result = jnp.zeros((8, LANES), f32)
    for h in range(2):
        for jt in range(8):

            def inner(i, sums):
                k = blocks[h, i, jt * 8 : jt * 8 + 8, :]
                return tuple(
                    s + k * jnp.broadcast_to(got[pl.ds(i * ROWS + h * 12 + r, 1), :], (8, LANES))
                    for r, s in enumerate(sums)
                )

            zero = jnp.zeros((8, LANES), f32)
            sums = (zero,) * 12
            if jt < 7:
                sums = lax.fori_loop(jt * 8 + 8, EB, inner, sums, unroll=4)
                sums = tuple(s + s for s in sums)
            sums = lax.fori_loop(jt * 8, jt * 8 + 8, inner, sums, unroll=4)
            for r in range(12):
                mine = got[pl.ds(jt * 8 * ROWS + h * 12 + r, 8, stride=ROWS), :]
                result = result + sums[r] * mine
    return result


def early_kernel(b_rows, w, moments):
    b = b_rows[0:24, :]
    moments[0:8, :] = fold(b * b)
    moments[8:16, :] = fold(b * w[...])
    moments[16:24, :] = fold(w[...] * w[...])


def third_kernel(freq, v, low, up, conn, hot, blocks, mass_row, w, early, got, line_out, stack):
    gather_blocks(v, low, up, conn, hot, stack, [(got, 0, ROWS)])
    last = quadratic(blocks, got)
    weights = edge_weights(freq, ROWS, 256)
    for t in range(8):
        cols = slice(t * 256, (t + 1) * 256)
        last = last + fold(weights * mass_row[0:1, cols] * v[:, cols] * v[:, cols])
    parts = [early[0:8, :], early[8:16, :], early[16:24, :], fold(w[...] * v[...]), fold(v[...] * v[...]), last]
    lane = lax.broadcasted_iota(i32, (1, LANES), 1)
    line = jnp.zeros((1, LANES), f32)
    for k, tile in enumerate(parts):
        line = line + jnp.where((lane & 7) == k, jnp.sum(tile), 0.0)
    line_out[...] = jnp.broadcast_to(line, (8, LANES))


def field_kernel(blocks, got, y):
    product(blocks, got, y, 2, 8, 4)


def gradients(got_rows, y, node_block, node_shape, energy, out, base):
    for jt in range(8):
        ys = [y[r * EB + jt * 8 : r * EB + jt * 8 + 8, :] for r in range(4)]
        for o in range(6):
            term = jnp.zeros((8, LANES), f32)
            for h in range(2):
                for c in range(2):
                    x = got_rows[pl.ds(jt * 8 * ROWS + h * 12 + o * 2 + c, 8, stride=ROWS), :]
                    term = term - x * ys[h * 2 + c] if c else term + x * ys[h * 2 + c]
            energy[o, jt * 8 : jt * 8 + 8, :] = term

    def body(c, carry):
        index = jnp.broadcast_to(node_block[pl.ds(c, 1), :], (8, LANES))
        cols = pl.ds(pl.multiple_of(c * LANES, LANES), LANES)
        sums = [jnp.zeros((8, LANES), f32) for _ in range(18)]
        for jt in range(8):
            shape = [node_shape[k, jt * 8 : jt * 8 + 8, cols] for k in range(3)]
            for o in range(6):
                x = jnp.take_along_axis(energy[o, jt * 8 : jt * 8 + 8, :], index, axis=1, mode="promise_in_bounds")
                for k in range(3):
                    sums[o * 3 + k] = sums[o * 3 + k] - shape[k] * x
        for q in range(18):
            out[c, base + q : base + q + 1, :] = jnp.sum(sums[q], axis=0, keepdims=True)
        return carry

    lax.fori_loop(0, 8, body, 0)


def early_gradient_kernel(got0, got1, y, node_block, node_shape, out, energy):
    gradients(got0, y, node_block, node_shape, energy, out, 0)
    gradients(got1, y, node_block, node_shape, energy, out, 18)
    out[:, 36:40, :] = jnp.zeros((8, 4, LANES), f32)


def late_gradient_kernel(early, got2, y, node_block, node_shape, line, out, energy):
    out[:, 0:40, :] = early[...]
    gradients(got2, y, node_block, node_shape, energy, out, 40)
    for c in range(8):
        out[c, 58:64, :] = line[0:6, :]


def message_kernel(shares, out):
    line = shares[0, 60:61, :]
    for d in range(1, 8):
        line = line + shares[d, 60:61, :]
    out[...] = jnp.broadcast_to(line, (32, LANES))


def last_kernel(messages, rows, w, v, shares, adjoint, gradient):
    line = jnp.sum(messages[...], axis=0, keepdims=True)
    lane = lax.broadcasted_iota(i32, (1, LANES), 1)

    def moment(k):
        return jnp.sum(jnp.where((lane & 7) == k, line, 0.0), axis=1, keepdims=True)

    m = [moment(k) for k in range(6)]
    a0 = m[0] / m[1]
    r1 = (None, -a0)
    rr1 = m[0] - 2.0 * a0 * m[1] + a0 * a0 * m[2]
    b0 = rr1 / m[0]
    d1 = (1.0 + b0, -a0)
    dad1 = d1[0] * d1[0] * m[1] + 2.0 * d1[0] * d1[1] * m[2] + d1[1] * d1[1] * m[3]
    a1 = rr1 / dad1
    r2 = (None, r1[1] - a1 * d1[0], -a1 * d1[1])
    rr2 = (
        m[0] + 2.0 * r2[1] * m[1] + (2.0 * r2[2] + r2[1] * r2[1]) * m[2]
        + 2.0 * r2[1] * r2[2] * m[3] + r2[2] * r2[2] * m[4]
    )
    b1 = rr2 / rr1
    d2 = (1.0 + b1 * d1[0], r2[1] + b1 * d1[1], r2[2])
    dad2 = (
        d2[0] * d2[0] * m[1] + 2.0 * d2[0] * d2[1] * m[2] + (2.0 * d2[0] * d2[2] + d2[1] * d2[1]) * m[3]
        + 2.0 * d2[1] * d2[2] * m[4] + d2[2] * d2[2] * m[5]
    )
    a2 = rr2 / dad2
    c0 = a0 + a1 * d1[0] + a2 * d2[0]
    c1 = a1 * d1[1] + a2 * d2[1]
    c2 = a2 * d2[2]
    for h in range(2):
        for o in range(6):
            at = slice(h * 12 + o * 2, h * 12 + o * 2 + 2)
            adjoint[h, o] = c0 * rows[at, :] + c1 * w[at, :] + c2 * v[at, :]
    share = shares[0]
    for d in range(1, 8):
        share = share + shares[d]
    for o in range(6):
        gradient[o] = (
            c0 * share[o * 3 : o * 3 + 3] + c1 * share[18 + o * 3 : 21 + o * 3] + c2 * share[40 + o * 3 : 43 + o * 3]
        )


def shifted(x, by):
    count = lax.axis_size("mesh")
    return lax.ppermute(x, "mesh", [(i, i + by) for i in range(count) if 0 <= i + by < count])


def exchanged(to_low, to_up):
    return shifted(to_up, 1), shifted(to_low, -1)


def per_device(
    adjoint_rhs, forward_field, stiffness, mass_blocks, frequency, edge_mass, connectivity, send_list, node_block, node_shape
):
    lists = send_list[0]
    mass_row = edge_mass.reshape(1, EDGES)
    nodes = node_block.reshape(8, LANES)
    ghosts = (arr(ROWS, SLOTS), arr(ROWS, SLOTS))
    got_shape = arr(EB * ROWS, LANES)
    medium = dict(flops=10**9, nbytes=10**7)

    rows, to_low, to_up = kernel_call(
        prep_kernel, "prep", (arr(32, EDGES), arr(32, SLOTS), arr(32, SLOTS)), [HBM] * 3,
        [
            pltpu.VMEM(adjoint_rhs.shape, f32),
            pltpu.VMEM(forward_field.shape, f32),
            pltpu.VMEM(lists.shape, i32),
            pltpu.SemaphoreType.DMA((3,)),
        ],
        flops=10**6, nbytes=10**6, limit=62,
    )(adjoint_rhs, forward_field, lists)
    low, up = exchanged(to_low, to_up)
    (hot,) = kernel_call(
        hot_kernel, "hot", (jax.ShapeDtypeStruct((WIDE, EB * LANES), bf16),), [VMEM], **medium
    )(connectivity)
    (blocks,) = kernel_call(blocks_kernel, "blocks", (arr(2, EB, EB, LANES),), [SMEM] + [VMEM] * 2, **medium)(
        frequency, stiffness, mass_blocks
    )

    def applied(x, low, up, with_field):
        count = 2 * PARTS * x.shape[0]
        p, to_low, to_up, *got = kernel_call(
            functools.partial(apply_kernel, with_field), "apply",
            (arr(ROWS, EDGES),) + ghosts + (got_shape,) + (arr(EB * 8, LANES),) * with_field, [SMEM] + [VMEM] * 7,
            [
                pltpu.VMEM((count, WIDE), bf16),
                pltpu.VMEM((ROWS * EB, LANES), f32),
                pltpu.VMEM((PARTS * 48, CHUNK * LANES), bf16),
                pltpu.VMEM((PARTS * 48, WIDE), f32),
            ],
            **medium,
        )(frequency, x, low, up, connectivity, hot, blocks, mass_row)
        from_low, from_up = exchanged(to_low, to_up)
        own, to_low, to_up = kernel_call(
            finish_kernel, "finish", (arr(ROWS, EDGES),) + ghosts, [VMEM] * 4, flops=10**7, nbytes=10**6
        )(p, lists, from_low, from_up)
        return got, own, exchanged(to_low, to_up)

    (got0, got_field), w, (low, up) = applied(rows, low, up, True)
    (y,) = kernel_call(field_kernel, "field", (arr(4 * EB, LANES),), [VMEM] * 2, **medium)(blocks, got_field)
    (got1,), v, (low, up) = applied(w, low, up, False)
    (grads,) = kernel_call(
        early_gradient_kernel, "early_gradient", (arr(8, 40, LANES),), [VMEM] * 5, [pltpu.VMEM((6, EB, LANES), f32)], **medium
    )(got0, got1, y, nodes, node_shape)
    (early,) = kernel_call(early_kernel, "early", (arr(24, LANES),), [VMEM] * 2, flops=10**6, nbytes=10**6)(rows, w)
    got2, line = kernel_call(
        third_kernel, "third", (got_shape, arr(8, LANES)), [SMEM] + [VMEM] * 9,
        [pltpu.VMEM((PARTS * 48, WIDE), bf16)], **medium,
    )(frequency, v, low, up, connectivity, hot, blocks, mass_row, w, early)
    (grads,) = kernel_call(
        late_gradient_kernel, "late_gradient", (arr(8, 64, LANES),), [VMEM] * 6, [pltpu.VMEM((6, EB, LANES), f32)], **medium
    )(grads, got2, y, nodes, node_shape, line)
    shares = lax.all_to_all(grads, "harm", 0, 0, tiled=True)
    (message,) = kernel_call(message_kernel, "message", (arr(32, LANES),), [VMEM], flops=10**3, nbytes=10**5)(shares)
    messages = lax.all_to_all(message.reshape(32 * LANES), "mesh", 0, 0, tiled=True).reshape(32, LANES)
    adjoint, gradient = kernel_call(
        last_kernel, "last", (arr(*adjoint_rhs.shape), arr(6, 3, LANES)), [VMEM] * 5, flops=10**6, nbytes=10**6
    )(messages, rows, w, v, shares)
    return adjoint, gradient


def solution(mesh):
    return jax.shard_map(
        per_device,
        mesh=mesh,
        in_specs=(
            P("harm", None, None, "mesh"),
            P("harm", None, "mesh"),
            P(None, None, "mesh"),
            P(None, None, "mesh"),
            P("harm"),
            P("mesh"),
            P(None, "mesh"),
            P("mesh", None, None),
            P("mesh"),
            P(None, None, "mesh"),
        ),
        out_specs=(P("harm", None, None, "mesh"), P(None, None, ("mesh", "harm"))),
        check_vma=False,
    )
```

```python
import functools

import jax
import jax.numpy as jnp
from jax import lax
from jax.experimental import pallas as pl
from jax.experimental.pallas import tpu as pltpu
from jax.sharding import PartitionSpec as P

f32 = jnp.float32
bf16 = jnp.bfloat16
i32 = jnp.int32
LANES = 128
EDGES = 2048
SLOTS = 512
ROWS = 24
EB = 64
OWN_T, GHOST_T = EDGES // LANES, SLOTS // LANES
BOTH = ("mesh", "harm")

VMEM = pl.BlockSpec(memory_space=pltpu.VMEM)
SMEM = pl.BlockSpec(memory_space=pltpu.SMEM)
HBM = pl.BlockSpec(memory_space=pltpu.HBM)


def kernel_call(body, name, out, specs, scratch=(), flops=0, nbytes=0, limit=20):
    return pl.pallas_call(
        body,
        name=name,
        out_shape=out,
        in_specs=specs,
        out_specs=jax.tree.map(lambda _: VMEM, out),
        scratch_shapes=scratch,
        compiler_params=pltpu.CompilerParams(vmem_limit_bytes=limit * 2**20),
        cost_estimate=pl.CostEstimate(flops=flops, bytes_accessed=nbytes, transcendentals=0),
    )


def arr(*shape):
    return jax.ShapeDtypeStruct(shape, f32)


def lookup(tables, index):
    lane = jnp.broadcast_to(index & (LANES - 1), (8, LANES))
    high = jnp.broadcast_to(index >> 7, (8, LANES))
    found = [jnp.take_along_axis(t, lane, axis=1, mode="promise_in_bounds") for t in tables]
    bit = 1
    while len(found) > 1:
        odd = (high & bit) != 0
        found = [
            jnp.where(odd, found[a + 1], found[a]) if a + 1 < len(found) else found[a]
            for a in range(0, len(found), 2)
        ]
        bit *= 2
    return found[0]


def tiles(ref, row, count):
    return [ref[row : row + 8, t * LANES : (t + 1) * LANES] for t in range(count)]


WIDE = 512
PARTS = (EDGES + 2 * SLOTS) // WIDE
CHUNK = 16


def gather_blocks(own, low, up, conn, hot, stack, outs):
    count = own.shape[0]
    for t in range(PARTS):
        x = own[:, t * WIDE : (t + 1) * WIDE] if t < PARTS - 2 else (low if t == PARTS - 2 else up)[...]
        stack[t * 2 * count : (t + 1) * 2 * count, :] = pieces(x)

    for c in range(EB // CHUNK):
        found = jnp.dot(stack[...], hot[:, c * CHUNK * LANES : (c + 1) * CHUNK * LANES], preferred_element_type=f32)
        for jj in range(CHUNK):
            j = c * CHUNK + jj
            high = conn[j : j + 1, :] >> 9
            for out, first, rows in outs:
                value = None
                for t in range(PARTS):
                    at = t * 2 * count + first
                    lanes = slice(jj * LANES, (jj + 1) * LANES)
                    x = found[at : at + rows, lanes] + found[at + count : at + count + rows, lanes]
                    value = x if t == 0 else jnp.where(jnp.broadcast_to(high, x.shape) == t, x, value)
                out[j * rows : (j + 1) * rows, :] = value


def product(blocks, got, out, per_harm, per_edge, wide):
    for h in range(2):

        def outer(jt, carry):
            def inner(i, sums):
                ks = []
                for q in range(wide):
                    rows = pl.ds((jt * wide + q) * 8, 8)
                    ks.append(blocks[h, i, rows, :])
                new = []
                for r in range(per_harm):
                    x = jnp.broadcast_to(got[pl.ds(i * per_edge + h * per_harm + r, 1), :], (8, LANES))
                    for q in range(wide):
                        new.append(sums[r * wide + q] + ks[q] * x)
                return tuple(new)

            zero = jnp.zeros((8, LANES), f32)
            sums = lax.fori_loop(0, EB, inner, (zero,) * (per_harm * wide), unroll=16)
            for r in range(per_harm):
                for q in range(wide):
                    at = (h * per_harm + r) * EB + (jt * wide + q) * 8
                    out[pl.ds(at, 8), :] = sums[r * wide + q]
            return carry

        for jt in range(EB // (8 * wide)):
            outer(jt, 0)


def pieces(x):
    high = x.astype(bf16).astype(f32)
    return jnp.concatenate([high, x - high], axis=0).astype(bf16)


def one_hot_low(index):
    low = jnp.broadcast_to(index & 255, (256, LANES))
    return jnp.where(low == lax.broadcasted_iota(i32, (256, LANES), 0), 1.0, 0.0).astype(bf16)


def masked_stack(parts, index, first, last):
    high = index >> 8
    stack = []
    for t in range(first, last):
        mask = jnp.broadcast_to(jnp.where(high == t, 1.0, 0.0), parts.shape).astype(bf16)
        stack.append(parts * mask)
    return stack


def add_up(stack, hot):
    return lax.dot_general(stack, hot, (((1,), (1,)), ((), ())), preferred_element_type=f32)


def scatter_blocks(terms, conn, hot, stack, total):
    total[...] = jnp.zeros_like(total)
    for c in range(EB // CHUNK):

        def body(jj, carry):
            j = c * CHUNK + jj
            cols = pl.ds(pl.multiple_of(jj * LANES, LANES), LANES)
            x = terms[pl.ds(j, ROWS, stride=EB), :]
            first = x.astype(bf16).astype(f32)
            rest = x - first
            high = jnp.broadcast_to(conn[pl.ds(j, 1), :] >> 9, (ROWS, LANES))
            for t in range(PARTS):
                here = high == t
                both = jnp.concatenate([jnp.where(here, first, 0.0), jnp.where(here, rest, 0.0)], axis=0)
                stack[t * 48 : t * 48 + 48, cols] = both.astype(bf16)
            return carry

        lax.fori_loop(0, CHUNK, body, 0, unroll=CHUNK)
        total[...] += add_up(stack[...], hot[:, c * CHUNK * LANES : (c + 1) * CHUNK * LANES])


def total_tile(total, t):
    return total[t * 48 : t * 48 + 24, :] + total[t * 48 + 24 : t * 48 + 48, :]


def edge_weights(freq, rows, width):
    upper = lax.broadcasted_iota(i32, (rows, width), 0) < rows // 2
    return jnp.where(upper, freq[0], freq[1])


def pick_listed(source, lists, outs, groups):
    for side in range(2):
        for c in range(GHOST_T):
            cols = slice(c * LANES, (c + 1) * LANES)
            index = lists[side : side + 1, cols]
            for g in range(groups):
                value = lookup(tiles(source, g * 8, OWN_T), index)
                outs[side][g * 8 : g * 8 + 8, cols] = jnp.where(index >= 0, value, 0.0)


def fold(x):
    rows, cols = x.shape
    total = jnp.zeros((8, LANES), f32)
    for r in range(rows // 8):
        for c in range(cols // LANES):
            total = total + x[r * 8 : r * 8 + 8, c * LANES : (c + 1) * LANES]
    return total


def prep_kernel(rhs_in, field_in, lists_in, rows, to_low, to_up, rhs, field, lists, sems):
    copies = [
        pltpu.make_async_copy(a, b, sems.at[k])
        for k, (a, b) in enumerate(((rhs_in, rhs), (field_in, field), (lists_in, lists)))
    ]
    for copy in copies:
        copy.start()
    for copy in copies:
        copy.wait()
    for h in range(2):
        for o in range(6):
            at = h * 12 + o * 2
            rows[at : at + 2, :] = rhs[h, o]
        rows[24 + 2 * h : 26 + 2 * h, :] = field[h]
    rows[28:32, :] = jnp.zeros((4, EDGES), f32)
    pick_listed(rows, lists, (to_low, to_up), 4)


def hot_kernel(conn, hot):
    half = WIDE // 2

    def body(j, carry):
        index = conn[pl.ds(j, 1), :]
        cols = pl.ds(pl.multiple_of(j * LANES, LANES), LANES)
        low = jnp.broadcast_to(index & (half - 1), (half, LANES))
        one = jnp.where(low == lax.broadcasted_iota(i32, (half, LANES), 0), 1.0, 0.0).astype(bf16)
        upper = jnp.broadcast_to(jnp.where((index & half) != 0, 1.0, 0.0), (16, LANES))
        upper, lower = upper.astype(bf16), (1.0 - upper).astype(bf16)
        for q in range(half // 16):
            part = one[q * 16 : q * 16 + 16]
            hot[q * 16 : q * 16 + 16, cols] = part * lower
            hot[half + q * 16 : half + q * 16 + 16, cols] = part * upper
        return carry

    lax.fori_loop(0, EB, body, 0, unroll=8)


def blocks_kernel(freq, stiff, mass, blocks):
    def body(i, carry):
        for h in range(2):
            blocks[h, i] = stiff[i] + freq[h] * mass[i]
        return carry

    lax.fori_loop(0, EB, body, 0, unroll=2)


def apply_kernel(with_field, freq, own, low, up, conn, hot, blocks, mass_row, p, to_low, to_up, got, *refs):
    stack, terms, masked, total = refs[-4:]
    outs = [(got, 0, ROWS)] + ([(refs[0], ROWS, 8)] if with_field else [])
    gather_blocks(own, low, up, conn, hot, stack, outs)
    product(blocks, got, terms, 12, ROWS, 2)
    scatter_blocks(terms, conn, hot, masked, total)
    weights = edge_weights(freq, ROWS, WIDE)
    for t in range(PARTS):
        sums = total[t * 48 : t * 48 + 24, :] + total[t * 48 + 24 : t * 48 + 48, :]
        if t < PARTS - 2:
            cols = slice(t * WIDE, (t + 1) * WIDE)
            p[:, cols] = sums + weights * mass_row[0:1, cols] * own[0:ROWS, cols]
        else:
            (to_low if t == PARTS - 2 else to_up)[...] = sums


def finish_kernel(p, lists, from_low, from_up, own, to_low, to_up):
    arrived = jnp.concatenate([from_low[...], from_up[...]], axis=1)
    hots, stacks = [], []
    for c in range(2 * GHOST_T):
        index = lists[c // GHOST_T : c // GHOST_T + 1, (c % GHOST_T) * LANES : (c % GHOST_T + 1) * LANES]
        hots.append(one_hot_low(index))
        parts = pieces(arrived[:, c * LANES : (c + 1) * LANES])
        stacks.append(jnp.concatenate(masked_stack(parts, index, 0, 8), axis=0))
    sums = add_up(jnp.concatenate(stacks, axis=1), jnp.concatenate(hots, axis=1))
    for t in range(8):
        own[:, t * 256 : (t + 1) * 256] = p[:, t * 256 : (t + 1) * 256] + total_tile(sums, t)
    pick_listed(own, lists, (to_low, to_up), 3)


def quadratic(blocks, got):
    result = jnp.zeros((8, LANES), f32)
    for h in range(2):
        for jt in range(8):

            def inner(i, sums):
                k = blocks[h, i, jt * 8 : jt * 8 + 8, :]
                return tuple(
                    s + k * jnp.broadcast_to(got[pl.ds(i * ROWS + h * 12 + r, 1), :], (8, LANES))
                    for r, s in enumerate(sums)
                )

            zero = jnp.zeros((8, LANES), f32)
            sums = (zero,) * 12
            if jt < 7:
                sums = lax.fori_loop(jt * 8 + 8, EB, inner, sums, unroll=4)
                sums = tuple(s + s for s in sums)
            sums = lax.fori_loop(jt * 8, jt * 8 + 8, inner, sums, unroll=4)
            for r in range(12):
                mine = got[pl.ds(jt * 8 * ROWS + h * 12 + r, 8, stride=ROWS), :]
                result = result + sums[r] * mine
    return result


def early_kernel(b_rows, w, moments):
    b = b_rows[0:24, :]
    moments[0:8, :] = fold(b * b)
    moments[8:16, :] = fold(b * w[...])
    moments[16:24, :] = fold(w[...] * w[...])


def third_kernel(freq, v, low, up, conn, hot, blocks, mass_row, w, early, got, line_out, stack):
    gather_blocks(v, low, up, conn, hot, stack, [(got, 0, ROWS)])
    last = quadratic(blocks, got)
    weights = edge_weights(freq, ROWS, 256)
    for t in range(8):
        cols = slice(t * 256, (t + 1) * 256)
        last = last + fold(weights * mass_row[0:1, cols] * v[:, cols] * v[:, cols])
    parts = [early[0:8, :], early[8:16, :], early[16:24, :], fold(w[...] * v[...]), fold(v[...] * v[...]), last]
    lane = lax.broadcasted_iota(i32, (1, LANES), 1)
    line = jnp.zeros((1, LANES), f32)
    for k, tile in enumerate(parts):
        line = line + jnp.where((lane & 7) == k, jnp.sum(tile), 0.0)
    line_out[...] = jnp.broadcast_to(line, (8, LANES))


def field_kernel(blocks, got, y):
    product(blocks, got, y, 2, 8, 4)


def gradients(got_rows, y, node_block, node_shape, energy, out, base):
    for jt in range(8):
        ys = [y[r * EB + jt * 8 : r * EB + jt * 8 + 8, :] for r in range(4)]
        for o in range(6):
            term = jnp.zeros((8, LANES), f32)
            for h in range(2):
                for c in range(2):
                    x = got_rows[pl.ds(jt * 8 * ROWS + h * 12 + o * 2 + c, 8, stride=ROWS), :]
                    term = term - x * ys[h * 2 + c] if c else term + x * ys[h * 2 + c]
            energy[o, jt * 8 : jt * 8 + 8, :] = term

    def body(c, carry):
        index = jnp.broadcast_to(node_block[pl.ds(c, 1), :], (8, LANES))
        cols = pl.ds(pl.multiple_of(c * LANES, LANES), LANES)
        sums = [jnp.zeros((8, LANES), f32) for _ in range(18)]
        for jt in range(8):
            shape = [node_shape[k, jt * 8 : jt * 8 + 8, cols] for k in range(3)]
            for o in range(6):
                x = jnp.take_along_axis(energy[o, jt * 8 : jt * 8 + 8, :], index, axis=1, mode="promise_in_bounds")
                for k in range(3):
                    sums[o * 3 + k] = sums[o * 3 + k] - shape[k] * x
        for q in range(18):
            out[c, base + q : base + q + 1, :] = jnp.sum(sums[q], axis=0, keepdims=True)
        return carry

    lax.fori_loop(0, 8, body, 0)


def early_gradient_kernel(got0, got1, y, node_block, node_shape, out, energy):
    gradients(got0, y, node_block, node_shape, energy, out, 0)
    gradients(got1, y, node_block, node_shape, energy, out, 18)
    out[:, 36:40, :] = jnp.zeros((8, 4, LANES), f32)


def late_gradient_kernel(early, got2, y, node_block, node_shape, line, out, energy):
    out[:, 0:40, :] = early[...]
    gradients(got2, y, node_block, node_shape, energy, out, 40)
    for c in range(8):
        out[c, 58:64, :] = line[0:6, :]


def message_kernel(shares, out):
    line = shares[0, 60:61, :]
    for d in range(1, 8):
        line = line + shares[d, 60:61, :]
    out[...] = jnp.broadcast_to(line, (32, LANES))


def last_kernel(messages, rows, w, v, shares, adjoint, gradient):
    line = jnp.sum(messages[...], axis=0, keepdims=True)
    lane = lax.broadcasted_iota(i32, (1, LANES), 1)

    def moment(k):
        return jnp.sum(jnp.where((lane & 7) == k, line, 0.0), axis=1, keepdims=True)

    m = [moment(k) for k in range(6)]
    a0 = m[0] / m[1]
    r1 = (None, -a0)
    rr1 = m[0] - 2.0 * a0 * m[1] + a0 * a0 * m[2]
    b0 = rr1 / m[0]
    d1 = (1.0 + b0, -a0)
    dad1 = d1[0] * d1[0] * m[1] + 2.0 * d1[0] * d1[1] * m[2] + d1[1] * d1[1] * m[3]
    a1 = rr1 / dad1
    r2 = (None, r1[1] - a1 * d1[0], -a1 * d1[1])
    rr2 = (
        m[0] + 2.0 * r2[1] * m[1] + (2.0 * r2[2] + r2[1] * r2[1]) * m[2]
        + 2.0 * r2[1] * r2[2] * m[3] + r2[2] * r2[2] * m[4]
    )
    b1 = rr2 / rr1
    d2 = (1.0 + b1 * d1[0], r2[1] + b1 * d1[1], r2[2])
    dad2 = (
        d2[0] * d2[0] * m[1] + 2.0 * d2[0] * d2[1] * m[2] + (2.0 * d2[0] * d2[2] + d2[1] * d2[1]) * m[3]
        + 2.0 * d2[1] * d2[2] * m[4] + d2[2] * d2[2] * m[5]
    )
    a2 = rr2 / dad2
    c0 = a0 + a1 * d1[0] + a2 * d2[0]
    c1 = a1 * d1[1] + a2 * d2[1]
    c2 = a2 * d2[2]
    for h in range(2):
        for o in range(6):
            at = slice(h * 12 + o * 2, h * 12 + o * 2 + 2)
            adjoint[h, o] = c0 * rows[at, :] + c1 * w[at, :] + c2 * v[at, :]
    share = shares[0]
    for d in range(1, 8):
        share = share + shares[d]
    for o in range(6):
        gradient[o] = (
            c0 * share[o * 3 : o * 3 + 3] + c1 * share[18 + o * 3 : 21 + o * 3] + c2 * share[40 + o * 3 : 43 + o * 3]
        )


def shifted(x, by):
    count = lax.axis_size("mesh")
    return lax.ppermute(x, "mesh", [(i, i + by) for i in range(count) if 0 <= i + by < count])


def exchanged(to_low, to_up):
    return shifted(to_up, 1), shifted(to_low, -1)


def per_device(
    adjoint_rhs, forward_field, stiffness, mass_blocks, frequency, edge_mass, connectivity, send_list, node_block, node_shape
):
    lists = send_list[0]
    mass_row = edge_mass.reshape(1, EDGES)
    nodes = node_block.reshape(8, LANES)
    ghosts = (arr(ROWS, SLOTS), arr(ROWS, SLOTS))
    got_shape = arr(EB * ROWS, LANES)
    medium = dict(flops=10**9, nbytes=10**7)

    rows, to_low, to_up = kernel_call(
        prep_kernel, "prep", (arr(32, EDGES), arr(32, SLOTS), arr(32, SLOTS)), [HBM] * 3,
        [
            pltpu.VMEM(adjoint_rhs.shape, f32),
            pltpu.VMEM(forward_field.shape, f32),
            pltpu.VMEM(lists.shape, i32),
            pltpu.SemaphoreType.DMA((3,)),
        ],
        flops=10**6, nbytes=10**6, limit=62,
    )(adjoint_rhs, forward_field, lists)
    low, up = exchanged(to_low, to_up)
    (hot,) = kernel_call(
        hot_kernel, "hot", (jax.ShapeDtypeStruct((WIDE, EB * LANES), bf16),), [VMEM], **medium
    )(connectivity)
    (blocks,) = kernel_call(blocks_kernel, "blocks", (arr(2, EB, EB, LANES),), [SMEM] + [VMEM] * 2, **medium)(
        frequency, stiffness, mass_blocks
    )

    def applied(x, low, up, with_field):
        count = 2 * PARTS * x.shape[0]
        p, to_low, to_up, *got = kernel_call(
            functools.partial(apply_kernel, with_field), "apply",
            (arr(ROWS, EDGES),) + ghosts + (got_shape,) + (arr(EB * 8, LANES),) * with_field, [SMEM] + [VMEM] * 7,
            [
                pltpu.VMEM((count, WIDE), bf16),
                pltpu.VMEM((ROWS * EB, LANES), f32),
                pltpu.VMEM((PARTS * 48, CHUNK * LANES), bf16),
                pltpu.VMEM((PARTS * 48, WIDE), f32),
            ],
            **medium,
        )(frequency, x, low, up, connectivity, hot, blocks, mass_row)
        from_low, from_up = exchanged(to_low, to_up)
        own, to_low, to_up = kernel_call(
            finish_kernel, "finish", (arr(ROWS, EDGES),) + ghosts, [VMEM] * 4, flops=10**7, nbytes=10**6
        )(p, lists, from_low, from_up)
        return got, own, exchanged(to_low, to_up)

    (got0, got_field), w, (low, up) = applied(rows, low, up, True)
    (y,) = kernel_call(field_kernel, "field", (arr(4 * EB, LANES),), [VMEM] * 2, **medium)(blocks, got_field)
    (got1,), v, (low, up) = applied(w, low, up, False)
    (grads,) = kernel_call(
        early_gradient_kernel, "early_gradient", (arr(8, 40, LANES),), [VMEM] * 5, [pltpu.VMEM((6, EB, LANES), f32)], **medium
    )(got0, got1, y, nodes, node_shape)
    (early,) = kernel_call(early_kernel, "early", (arr(24, LANES),), [VMEM] * 2, flops=10**6, nbytes=10**6)(rows, w)
    got2, line = kernel_call(
        third_kernel, "third", (got_shape, arr(8, LANES)), [SMEM] + [VMEM] * 9,
        [pltpu.VMEM((PARTS * 48, WIDE), bf16)], **medium,
    )(frequency, v, low, up, connectivity, hot, blocks, mass_row, w, early)
    (grads,) = kernel_call(
        late_gradient_kernel, "late_gradient", (arr(8, 64, LANES),), [VMEM] * 6, [pltpu.VMEM((6, EB, LANES), f32)], **medium
    )(grads, got2, y, nodes, node_shape, line)
    shares = lax.all_to_all(grads, "harm", 0, 0, tiled=True)
    (message,) = kernel_call(message_kernel, "message", (arr(32, LANES),), [VMEM], flops=10**3, nbytes=10**5)(shares)
    messages = lax.all_to_all(message.reshape(32 * LANES), "mesh", 0, 0, tiled=True).reshape(32, LANES)
    adjoint, gradient = kernel_call(
        last_kernel, "last", (arr(*adjoint_rhs.shape), arr(6, 3, LANES)), [VMEM] * 5, flops=10**6, nbytes=10**6
    )(messages, rows, w, v, shares)
    return adjoint, gradient


def solution(mesh):
    return jax.shard_map(
        per_device,
        mesh=mesh,
        in_specs=(
            P("harm", None, None, "mesh"),
            P("harm", None, "mesh"),
            P(None, None, "mesh"),
            P(None, None, "mesh"),
            P("harm"),
            P("mesh"),
            P(None, "mesh"),
            P("mesh", None, None),
            P("mesh"),
            P(None, None, "mesh"),
        ),
        out_specs=(P("harm", None, None, "mesh"), P(None, None, ("mesh", "harm"))),
        check_vma=False,
    )
```
